32 devices in a mesh: ctx: 8 (over z, y), exp: 4 (over x, core).
Axes of the slice: x: 2, y: 2, z: 4, core: 2. Of those that a mesh axis runs over, the one named last changes fastest.
Arguments:
- tokens: bfloat16 [1024, 4096], P('ctx'), may hold values from -6 to 6
- ada_shift: float32 [4096], replicated, may hold values from -3 to 3
- ada_scale: float32 [4096], replicated, may hold values from -3 to 3
- ada_gate: float32 [4096], replicated, may hold values from -6 to 6
- router: bfloat16 [4, 4096, 2], P('exp'), may hold values from -0.09375 to 0.09375
- expert_up: bfloat16 [4, 4096, 16384], P('exp', None, 'ctx'), may hold values from -0.09375 to 0.09375
- expert_down: bfloat16 [4, 16384, 4096], P('exp', 'ctx'), may hold values from -0.0625 to 0.0625
- picked_ids: int32 [4, 2, 32], P('exp'), may hold values from 0 to 1023, as said below
- out_grad: bfloat16 [1024, 4096], P('ctx'), may hold values from -6 to 6
Outputs:
- block_out: bfloat16 [1024, 4096], P('ctx')
- tokens_grad: bfloat16 [1024, 4096], P('ctx')
- up_grad: bfloat16 [4, 4096, 16384], P('exp', None, 'ctx')
- down_grad: bfloat16 [4, 16384, 4096], P('exp', 'ctx')
- router_grad: float32 [4, 4096, 2], P('exp')
- shift_grad: float32 [4096], replicated
- scale_grad: float32 [4096], replicated
- gate_grad: float32 [4096], replicated
The draws below stay inside these ranges and needn't reach their ends.
Inputs may be any that keep to these rules, and one draw needn't show every extreme that they name: Row picked_ids[e, j] lists 32 distinct tokens for expert e * 2 + j. Among the 128 tokens of any one index of ctx it picks at most 8, and for each expert exactly 8 from at least one such index.
All inputs are finite; a program needn't handle non-finite values.
Results may differ from the reference program's by a relative error of at most 0.007.
Values may be sent and summed in bfloat16 or wider, within the bound.
No kernel may reach another device: no remote copies, remote signals or barrier semaphores. Data moves between devices by JAX's collectives and lax.ppermute only.
A program may use at most 128 MiB of HBM per device.

```python
import jax
import jax.numpy as jnp
from jax import lax

D = 4096
HID = 8192
PAIR = 2
TOK_DEV = 128
MOST = 8
TOKENS = 1024
CAP = 32
N_CTX = 8
N_EXP = 4


def draw_picked_ids(key, part):
    slot_total = N_CTX * MOST

    def one_expert(expert_key):
        key_full, key_rank, key_tok = jax.random.split(expert_key, 3)
        full_shard = jax.random.randint(key_full, (), 0, N_CTX)
        ranking = jax.random.permutation(key_rank, slot_total).astype(jnp.int32)
        shard_of = jnp.arange(slot_total, dtype=jnp.int32) // MOST
        within = jnp.arange(slot_total, dtype=jnp.int32) % MOST
        scores = jnp.where(shard_of == full_shard, -1, ranking)
        chosen_slots = jnp.argsort(scores, stable=True)[:CAP]
        shard_keys = jax.random.split(key_tok, N_CTX)
        shuffles = jax.vmap(lambda each_key: jax.random.permutation(each_key, TOK_DEV))(shard_keys).astype(jnp.int32)
        token_ids = shard_of * TOK_DEV + shuffles[shard_of, within]
        return token_ids[chosen_slots].astype(jnp.int32)
    expert_keys = jax.random.split(jax.random.fold_in(key, 7), N_EXP * PAIR)
    return jax.vmap(one_expert)(expert_keys).reshape(N_EXP, PAIR, CAP)


def shard_levels(rng, extent, cuts, smallest, largest):
    gain = 1.0
    for position, blocks in cuts:
        heights = jax.random.uniform(jax.random.fold_in(jax.random.fold_in(rng, 6), position), (blocks,), jnp.float32, smallest / len(cuts), largest / len(cuts))
        gain = gain * jnp.repeat(jnp.exp(heights), extent[position] // blocks).reshape((-1,) + (1,) * (len(extent) - 1 - position))
    return gain


def scatter_about(key, shape, scale, most, cuts=(), kind=jnp.bfloat16):
    drawn = jax.random.normal(key, shape, jnp.float32) * scale
    if len(cuts) > 0:
        drawn = shard_levels(key, shape, cuts, -0.22, 0.18) * drawn
    return jnp.clip(drawn, min=-most, max=most).astype(kind)


def setup_inputs(seed: int = 0) -> dict:
    splits = jax.random.split(jax.random.key(seed), 10)
    tokens = scatter_about(splits[0], (TOKENS, D), 1.0, 6.0, ((0, 8),))
    ada_shift = scatter_about(splits[1], (D,), 0.5, 3.0, (), jnp.float32)
    ada_scale = scatter_about(splits[2], (D,), 0.5, 3.0, (), jnp.float32)
    ada_gate = scatter_about(splits[3], (D,), 1.5, 6.0, (), jnp.float32)
    router = scatter_about(splits[4], (N_EXP, D, PAIR), D ** -0.5, 0.09375, ((0, 4),))
    expert_up = scatter_about(splits[5], (N_EXP, D, PAIR * HID), D ** -0.5, 0.09375, ((0, 4), (2, 8)))
    expert_down = scatter_about(splits[6], (N_EXP, PAIR * HID, D), HID ** -0.5, 0.0625, ((0, 4), (1, 8)))
    picked_ids = draw_picked_ids(jax.random.fold_in(splits[9], 71), 0)
    out_grad = scatter_about(splits[8], (TOKENS, D), 1.0, 6.0, ((0, 8),))
    return dict(tokens=tokens, ada_shift=ada_shift, ada_scale=ada_scale, ada_gate=ada_gate, router=router, expert_up=expert_up, expert_down=expert_down, picked_ids=picked_ids, out_grad=out_grad)


GELU_C = 0.7978845608028654

def gelu_tanh(values):
    inner_arg = GELU_C * (values + 0.044715 * values * values * values)
    return 0.5 * values * (1.0 + jnp.tanh(inner_arg))

def gelu_slope(values):
    inner_arg = GELU_C * (values + 0.044715 * values * values * values)
    tangent = jnp.tanh(inner_arg)
    return 0.5 * (1.0 + tangent) + 0.5 * values * (1.0 - tangent * tangent) * GELU_C * (1.0 + 3.0 * 0.044715 * values * values)

def reference(tokens, ada_shift, ada_scale, ada_gate, router, expert_up, expert_down, picked_ids, out_grad):
    inputs = tokens.astype(jnp.float32)
    centered = inputs - lax.optimization_barrier(jnp.mean(inputs, axis=1, keepdims=True))
    inverse_std = lax.rsqrt(lax.optimization_barrier(jnp.mean(centered * centered, axis=1, keepdims=True)) + 1e-06)
    normed = centered * inverse_std
    hidden = (normed * (1.0 + ada_scale) + ada_shift).astype(jnp.bfloat16)
    mixture = jnp.zeros((TOKENS, D), jnp.float32)
    stored = []
    for owner_idx in range(N_EXP):
        for slot_index in range(PAIR):
            token_ids = picked_ids[owner_idx, slot_index]
            column = router[owner_idx, :, slot_index]
            row_block = hidden[token_ids]
            logits = jnp.dot(row_block, column, preferred_element_type=jnp.float32)
            weights = jax.nn.sigmoid(logits)
            up_block = expert_up[owner_idx][:, slot_index * HID:(slot_index + 1) * HID]
            down_block = expert_down[owner_idx][slot_index * HID:(slot_index + 1) * HID]
            pre_act = jnp.dot(row_block, up_block, preferred_element_type=jnp.float32)
            activated = gelu_tanh(pre_act).astype(jnp.bfloat16)
            expert_out = jnp.dot(activated, down_block, preferred_element_type=jnp.float32)
            mixture = mixture.at[token_ids].add(weights[:, None] * expert_out)
            stored.append((token_ids, column, weights, row_block, up_block, down_block, pre_act, activated, expert_out))
    block_out = (inputs + ada_gate * mixture).astype(jnp.bfloat16)
    grad_in = out_grad.astype(jnp.float32)
    grad_mix = ada_gate * grad_in
    gate_grad = lax.optimization_barrier(jnp.sum(grad_in * mixture, axis=0))
    grad_hidden = jnp.zeros((TOKENS, D), jnp.float32)
    up_list = []
    down_list = []
    router_list = []
    for owner_idx in range(N_EXP):
        up_parts = []
        down_parts = []
        router_parts = []
        for slot_index in range(PAIR):
            token_ids, column, weights, row_block, up_block, down_block, pre_act, activated, expert_out = stored[owner_idx * PAIR + slot_index]
            mix_rows = grad_mix[token_ids]
            grad_rows = (weights[:, None] * mix_rows).astype(jnp.bfloat16)
            grad_weight = lax.optimization_barrier(jnp.sum(mix_rows * expert_out, axis=1))
            grad_logit = grad_weight * weights * (1.0 - weights)
            grad_act = jnp.dot(grad_rows, down_block.T, preferred_element_type=jnp.float32)
            grad_pre = (grad_act * gelu_slope(pre_act)).astype(jnp.bfloat16)
            down_parts.append(jnp.dot(activated.T, grad_rows, preferred_element_type=jnp.float32).astype(jnp.bfloat16))
            up_parts.append(jnp.dot(row_block.T, grad_pre, preferred_element_type=jnp.float32).astype(jnp.bfloat16))
            back_sum = jnp.dot(grad_pre, up_block.T, preferred_element_type=jnp.float32)
            grad_hidden = grad_hidden.at[token_ids].add(back_sum + grad_logit[:, None] * column.astype(jnp.float32)[None, :])
            router_parts.append(lax.optimization_barrier(jnp.sum(grad_logit[:, None] * row_block.astype(jnp.float32), axis=0)))
        up_list.append(jnp.concatenate(up_parts, axis=1))
        down_list.append(jnp.concatenate(down_parts, axis=0))
        router_list.append(jnp.stack(router_parts, axis=1))
    shift_grad = lax.optimization_barrier(jnp.sum(grad_hidden, axis=0))
    scale_grad = lax.optimization_barrier(jnp.sum(grad_hidden * normed, axis=0))
    grad_norm = grad_hidden * (1.0 + ada_scale)
    tokens_grad = (grad_in + inverse_std * (grad_norm - lax.optimization_barrier(jnp.mean(grad_norm, axis=1, keepdims=True)) - normed * lax.optimization_barrier(jnp.mean(grad_norm * normed, axis=1, keepdims=True)))).astype(jnp.bfloat16)
    up_grad = jnp.stack(up_list)
    down_grad = jnp.stack(down_list)
    router_grad = jnp.stack(router_list)
    return (block_out, tokens_grad, up_grad, down_grad, router_grad, shift_grad, scale_grad, gate_grad)
```

```python
import functools

import jax
import jax.numpy as jnp
from jax import lax
from jax.experimental import pallas as pl
from jax.experimental.pallas import tpu as pltpu
from jax.sharding import PartitionSpec as P

MOST = 8
GROUP = 2 * MOST
SIDE = 8
GELU_C = 0.7978845608028654
MIB = 1 << 20
f32, bf16 = jnp.float32, jnp.bfloat16
WHOLE = pl.BlockSpec(memory_space=pltpu.VMEM)
SCALARS = pl.BlockSpec(memory_space=pltpu.SMEM)


def dot(left, right, left_dim, right_dim):
    return lax.dot_general(
        left, right, (((left_dim,), (right_dim,)), ((), ())), preferred_element_type=f32
    )


def iota(shape, dim):
    return lax.broadcasted_iota(jnp.int32, shape, dim)


def select_body(place, picked, tokens, grads, own_o, other_o, ids_o):
    tok_count = tokens.shape[0]
    cap = picked.shape[1]
    start = place[0] * tok_count
    group = place[1]
    ids = picked[...].astype(f32)
    lanes, rows = iota((cap, cap), 1), iota((cap, cap), 0)
    eye = (lanes == rows).astype(f32)
    before = (rows < lanes).astype(f32)
    slot = (iota((GROUP, cap), 0) % MOST).astype(f32)
    tables = []
    for which in range(2):
        row = jnp.where(group == which, ids[0:1], ids[1:2]) - start.astype(f32)
        inside = ((row >= 0.0) & (row < float(tok_count))).astype(f32)
        inside_col = jnp.sum(eye * inside, axis=1, keepdims=True)
        local_col = jnp.sum(eye * row, axis=1, keepdims=True)
        rank = jnp.sum(before * inside_col, axis=0, keepdims=True)
        hit = jnp.where(rank == slot, 1.0, 0.0) * inside
        token_hit = (local_col == iota((cap, tok_count), 1).astype(f32)).astype(f32)
        tables.append(dot(hit, token_hit, 1, 0))
    table = jnp.concatenate(tables, axis=0).astype(bf16)
    second = (iota((2 * GROUP, 1), 0) % GROUP) >= MOST
    rows = jnp.where(second, dot(table, grads[...], 1, 0), dot(table, tokens[...], 1, 0)).astype(bf16)
    own_o[...] = rows[:GROUP]
    other_o[...] = rows[GROUP:]
    number = (iota((SIDE, tok_count), 1) + 1).astype(bf16)
    ids_row = dot(number, table, 1, 1) - 1.0
    kind = (iota((SIDE, 2 * GROUP), 1) % GROUP) >= MOST
    want = iota((SIDE, 2 * GROUP), 0) == 1
    ids_o[...] = jnp.where(kind == want, ids_row, -1.0)


def select(place, picked, tokens, grads):
    width = tokens.shape[1]
    return pl.pallas_call(
        select_body,
        in_specs=[SCALARS, WHOLE, WHOLE, WHOLE],
        out_specs=[WHOLE, WHOLE, WHOLE],
        out_shape=[
            jax.ShapeDtypeStruct((GROUP, width), bf16),
            jax.ShapeDtypeStruct((GROUP, width), bf16),
            jax.ShapeDtypeStruct((SIDE, 2 * GROUP), f32),
        ],
        compiler_params=pltpu.CompilerParams(vmem_limit_bytes=16 * MIB),
        name="select",
    )(place, picked, tokens, grads)


def expert_body(
    steps, blocks, counts, near, far, shift, scale, gate, column, up, down,
    hid_o, grows_o, act_o, gpre_o, keep_o, send_o, normed_s, eo_s, back_s, weight_s,
):
    index = pl.program_id(0)
    width = hid_o.shape[1]
    chunk = up.shape[2]
    half = blocks // 2

    def slots(block):
        source = near if block < half else far
        at = GROUP * (block % half)
        parts = [source[at + GROUP * k : at + GROUP * (k + 1), :].astype(f32) for k in range(2)]
        return [jnp.concatenate([p[k * MOST : (k + 1) * MOST] for p in parts], axis=0) for k in range(2)]

    @pl.when(index == 0)
    def _():
        one = 1.0 + scale[...]
        place = iota((GROUP, 1), 0)
        for block in range(0, blocks, 2):
            tok, grd = slots(block)
            rows = pl.ds(block * MOST, GROUP)
            limit = jnp.where(place < MOST, counts[block], counts[block + 1] + MOST)
            filled = (place < limit).astype(f32)
            centered = tok - jnp.mean(tok, axis=1, keepdims=True)
            inverse_std = lax.rsqrt(jnp.mean(centered * centered, axis=1, keepdims=True) + 1e-06)
            normed = centered * inverse_std
            normed_s[rows, :] = normed
            hidden = ((normed * one + shift[...]) * filled).astype(bf16)
            hid_o[rows, :] = hidden
            logit = jnp.sum(hidden.astype(f32) * column[...], axis=1, keepdims=True)
            weight = 1.0 / (1.0 + jnp.exp(-logit))
            weight_s[rows, :] = jnp.broadcast_to(weight, (GROUP, 128))
            grows_o[rows, :] = (weight * (gate[...] * grd)).astype(bf16)
        eo_s[...] = jnp.zeros_like(eo_s)
        back_s[...] = jnp.zeros_like(back_s)

    up_block, down_block = up[0], down[0]
    pre = dot(hid_o[...], up_block, 1, 0)
    grad_act = dot(grows_o[...], down_block, 1, 1)
    square = pre * pre
    tangent = jnp.tanh(GELU_C * (pre + 0.044715 * square * pre))
    act = (0.5 * pre * (1.0 + tangent)).astype(bf16)
    slope = 0.5 * (1.0 + tangent) + 0.5 * pre * (1.0 - tangent * tangent) * GELU_C * (
        1.0 + 3.0 * 0.044715 * square
    )
    grad_pre = (grad_act * slope).astype(bf16)
    here = pl.ds(pl.multiple_of(index * chunk, chunk), chunk)
    act_o[:, here] = act
    gpre_o[:, here] = grad_pre
    eo_s[...] += dot(act, down_block, 1, 0)
    back_s[...] += dot(grad_pre, up_block, 1, 1)

    @pl.when(index == steps - 1)
    def _():
        gate_v = shift_v = scale_v = router_v = jnp.zeros((1, width), f32)
        for block in range(0, blocks, 2):
            _, grd = slots(block)
            rows = pl.ds(block * MOST, GROUP)
            weight = weight_s[rows, 0:1]
            eo = eo_s[rows, :]
            grad_logit = jnp.sum(gate[...] * grd * eo, axis=1, keepdims=True) * weight * (1.0 - weight)
            eo = weight * eo
            back = back_s[rows, :] + grad_logit * column[...]
            gate_v += jnp.sum(grd * eo, axis=0, keepdims=True)
            shift_v += jnp.sum(back, axis=0, keepdims=True)
            scale_v += jnp.sum(back * normed_s[rows, :], axis=0, keepdims=True)
            router_v += jnp.sum(grad_logit * hid_o[rows, :].astype(f32), axis=0, keepdims=True)
            for k in range(2):
                cut = slice(k * MOST, (k + 1) * MOST)
                pair = jnp.concatenate([eo[cut], back[cut]], axis=0)
                at = GROUP * ((block + k) % half)
                if block < half:
                    keep_o[at : at + GROUP, :] = pair
                else:
                    send_o[at : at + GROUP, :] = pair.astype(bf16)
        side = jnp.concatenate([gate_v, shift_v, scale_v, router_v, jnp.zeros((SIDE - 4, width), f32)], axis=0)
        at = GROUP * half
        keep_o[at : at + SIDE, :] = side
        send_o[at : at + GROUP, :] = jnp.concatenate([side, jnp.zeros_like(side)], axis=0).astype(bf16)


def experts(counts, near, far, shift, scale, gate, column, up, down):
    blocks = counts.shape[0]
    slot_count = blocks * MOST
    width, hid_count = up.shape[1], up.shape[2]
    chunk = min(256, hid_count)
    steps = hid_count // chunk
    rows = GROUP * blocks // 2
    return pl.pallas_call(
        functools.partial(expert_body, steps, blocks),
        grid=(steps,),
        in_specs=[SCALARS] + [WHOLE] * 6
        + [
            pl.BlockSpec((1, width, chunk), lambda i: (0, 0, i)),
            pl.BlockSpec((1, chunk, width), lambda i: (0, i, 0)),
        ],
        out_specs=[WHOLE] * 6,
        out_shape=[
            jax.ShapeDtypeStruct((slot_count, width), bf16),
            jax.ShapeDtypeStruct((slot_count, width), bf16),
            jax.ShapeDtypeStruct((slot_count, hid_count), bf16),
            jax.ShapeDtypeStruct((slot_count, hid_count), bf16),
            jax.ShapeDtypeStruct((rows + SIDE, width), f32),
            jax.ShapeDtypeStruct((rows + GROUP, width), bf16),
        ],
        scratch_shapes=[pltpu.VMEM((slot_count, width), f32)] * 3 + [pltpu.VMEM((slot_count, 128), f32)],
        compiler_params=pltpu.CompilerParams(vmem_limit_bytes=32 * MIB),
        cost_estimate=pl.CostEstimate(
            flops=8 * slot_count * width * hid_count, bytes_accessed=4 * width * hid_count, transcendentals=0
        ),
        name="experts",
    )(counts, near, far, shift, scale, gate, column, up, down)


def outer_body(left, right, out):
    out[0] = dot(left[...], right[...], 0, 0).astype(bf16)


def outer(left, right, name):
    depth, rows = left.shape
    columns = right.shape[1]
    step = min(rows, 2 * MIB // columns)
    return pl.pallas_call(
        outer_body,
        grid=(rows // step,),
        in_specs=[pl.BlockSpec((depth, step), lambda i: (0, i)), WHOLE],
        out_specs=pl.BlockSpec((1, step, columns), lambda i: (0, i, 0)),
        out_shape=jax.ShapeDtypeStruct((1, rows, columns), bf16),
        compiler_params=pltpu.CompilerParams(vmem_limit_bytes=24 * MIB),
        cost_estimate=pl.CostEstimate(
            flops=8 * depth * rows * columns, bytes_accessed=4 * rows * columns, transcendentals=0
        ),
        name=name,
    )(left, right)


def finish_body(own, recv, scale, gate, tokens, grads, block_o, tgrad_o, gate_o, shift_o, scale_o):
    count = tokens.shape[0]
    start = pl.program_id(0) * count
    numbers = (iota((count, 2 * GROUP), 0) + start).astype(f32)
    pieces = [(part, k) for part in (own, recv) for k in range(own.shape[0])]
    rows = jnp.concatenate([part[k, : 2 * GROUP, :] for part, k in pieces], axis=0)
    tables = [[], []]
    for part, k in pieces:
        ids = part[k, 2 * GROUP :, : 2 * GROUP].astype(f32)
        for kind in range(2):
            tables[kind].append((numbers == ids[3 + kind : 4 + kind]).astype(f32))
    mixture, grad_hidden = [dot(jnp.concatenate(t, axis=1).astype(bf16), rows, 1, 0) for t in tables]
    inputs = tokens[...].astype(f32)
    block_o[...] = (inputs + gate[...] * mixture).astype(bf16)
    centered = inputs - jnp.mean(inputs, axis=1, keepdims=True)
    inverse_std = lax.rsqrt(jnp.mean(centered * centered, axis=1, keepdims=True) + 1e-06)
    normed = centered * inverse_std
    grad_norm = grad_hidden * (1.0 + scale[...])
    tgrad_o[...] = (
        grads[...].astype(f32)
        + inverse_std
        * (
            grad_norm
            - jnp.mean(grad_norm, axis=1, keepdims=True)
            - normed * jnp.mean(grad_norm * normed, axis=1, keepdims=True)
        )
    ).astype(bf16)

    @pl.when(pl.program_id(0) == 0)
    def _():
        side = sum(part[k, 2 * GROUP :, :].astype(f32) for part, k in pieces)
        gate_o[...] = side[0:1]
        shift_o[...] = side[1:2]
        scale_o[...] = side[2:3]


def finish(own, recv, scale, gate, tokens, grads):
    tok_count, width = tokens.shape
    step = min(tok_count, 32)
    block = pl.BlockSpec((step, width), lambda i: (i, 0))
    vector = jax.ShapeDtypeStruct((1, width), f32)
    return pl.pallas_call(
        finish_body,
        grid=(tok_count // step,),
        in_specs=[WHOLE] * 4 + [block, block],
        out_specs=[block, block] + [WHOLE] * 3,
        out_shape=[jax.ShapeDtypeStruct((tok_count, width), bf16)] * 2 + [vector] * 3,
        compiler_params=pltpu.CompilerParams(vmem_limit_bytes=16 * MIB),
        name="finish",
    )(own, recv, scale, gate, tokens, grads)


def swap(values, axis, mask):
    size = lax.axis_size(axis)
    return lax.ppermute(values, axis, [(i, i ^ mask) for i in range(size)])


def halvings(size):
    masks = []
    while size > 1:
        size //= 2
        masks.append(size)
    return masks


def per_device(
    tokens, ada_shift, ada_scale, ada_gate, router, expert_up, expert_down, picked_ids, out_grad
):
    tok_count, width = tokens.shape
    ctx_size, exp_size = lax.axis_size("ctx"), lax.axis_size("exp")
    ctx_masks, exp_masks = halvings(ctx_size), halvings(exp_size)
    me = lax.axis_index("ctx")
    group = me // ctx_masks[0]
    picked = picked_ids[0]
    shift, scale, gate = ada_shift[None], ada_scale[None], ada_gate[None]
    place = jnp.stack([me, group]).astype(jnp.int32)
    own, other, ids = select(place, picked, tokens, out_grad)

    relative = [0]
    for mask in ctx_masks:
        relative = relative + [r ^ mask for r in relative]
    sources = me ^ jnp.array(relative, jnp.int32)
    own_ids = jnp.where(group == 0, picked[0], picked[1])
    counts = jnp.sum((own_ids // tok_count)[None, :] == sources[:, None], axis=1).astype(jnp.int32)
    columns = router[0].astype(f32).T
    column = jnp.where(group == 0, columns[0:1], columns[1:2])

    near, far = own, swap(other, "ctx", ctx_masks[0])
    for mask in ctx_masks[1:]:
        near = jnp.concatenate([near, far], axis=0)
        far = swap(near, "ctx", mask)
    hidden, grad_rows, act, grad_pre, keep, send = experts(
        counts, near, far, shift, scale, gate, column, expert_up, expert_down
    )

    rows = keep.shape[0] - SIDE
    blocks, side = keep[:rows], keep[rows:]
    send = send[: rows + SIDE]
    for mask in ctx_masks[:0:-1]:
        got = swap(send, "ctx", mask).astype(f32)
        blocks, side = blocks + got[:rows], side + got[rows:]
        rows //= 2
        send = jnp.concatenate([blocks[rows:], side], axis=0).astype(bf16)
        blocks = blocks[:rows]
    got = swap(send, "ctx", ctx_masks[0]).astype(f32)
    theirs = got[rows:]
    router_rows = jnp.where(
        group == 0, jnp.stack([side[3], theirs[3]], axis=1), jnp.stack([theirs[3], side[3]], axis=1)
    )
    mine = jnp.concatenate(
        [blocks, got[:rows], side[:3] + theirs[:3], jnp.pad(ids[:2], ((0, 3), (0, width - ids.shape[1])))],
        axis=0,
    ).astype(bf16)[None]
    far = swap(mine, "exp", exp_masks[0])
    for mask in exp_masks[1:]:
        mine = jnp.concatenate([mine, far], axis=0)
        far = swap(mine, "exp", mask)

    up_grad = outer(hidden, grad_pre, "up_grad")
    down_grad = outer(act, grad_rows, "down_grad")
    block_out, tokens_grad, gate_grad, shift_grad, scale_grad = finish(
        mine, far, scale, gate, tokens, out_grad
    )
    return (
        block_out,
        tokens_grad,
        up_grad,
        down_grad,
        router_rows[None],
        shift_grad[0],
        scale_grad[0],
        gate_grad[0],
    )


def solution(mesh):
    in_specs = (
        P("ctx", None),
        P(),
        P(),
        P(),
        P("exp", None, None),
        P("exp", None, "ctx"),
        P("exp", "ctx", None),
        P("exp", None, None),
        P("ctx", None),
    )
    out_specs = (
        P("ctx", None),
        P("ctx", None),
        P("exp", None, "ctx"),
        P("exp", "ctx", None),
        P("exp", None, None),
        P(),
        P(),
        P(),
    )
    return jax.shard_map(
        per_device, mesh=mesh, in_specs=in_specs, out_specs=out_specs, check_vma=False
    )
```

```python
import functools

import jax
import jax.numpy as jnp
from jax import lax
from jax.experimental import pallas as pl
from jax.experimental.pallas import tpu as pltpu
from jax.sharding import PartitionSpec as P

MOST = 8
GROUP = 2 * MOST
PARTS = 4
SIDE = 8
GELU_C = 0.7978845608028654
MIB = 1 << 20
f32, bf16 = jnp.float32, jnp.bfloat16
WHOLE = pl.BlockSpec(memory_space=pltpu.VMEM)
SCALARS = pl.BlockSpec(memory_space=pltpu.SMEM)
ORDER = pl.BlockSpec(memory_space=pl.ANY)


def in_hbm(*arrays):
    return [pltpu.with_memory_space_constraint(array, pltpu.HBM) for array in arrays]


def start_copies(pairs, sems):
    copies = [pltpu.make_async_copy(a, b, sems.at[k]) for k, (a, b) in enumerate(pairs)]
    for copy in copies:
        copy.start()
    return copies


def dot(left, right, left_dim, right_dim):
    return lax.dot_general(
        left, right, (((left_dim,), (right_dim,)), ((), ())), preferred_element_type=f32
    )


def iota(shape, dim):
    return lax.broadcasted_iota(jnp.int32, shape, dim)


def select_body(place, picked_h, tokens_h, grads_h, own_o, other_o, ids_o, picked, tokens, grads, sems):
    tok_count = tokens.shape[0]
    pairs = [(picked_h, picked)]
    for k in range(PARTS):
        cut = pl.ds(k * (tok_count // PARTS), tok_count // PARTS)
        pairs += [(tokens_h.at[cut], tokens.at[cut]), (grads_h.at[cut], grads.at[cut])]
    copies = start_copies(pairs, sems)
    cap = picked.shape[2]
    start = place[0] * tok_count
    group = place[1]
    copies[0].wait()
    ids = picked[0].astype(f32)
    lanes, rows = iota((cap, cap), 1), iota((cap, cap), 0)
    eye = (lanes == rows).astype(f32)
    before = (rows < lanes).astype(f32)
    slot = (iota((GROUP, cap), 0) % MOST).astype(f32)
    tables = []
    for which in range(2):
        row = jnp.where(group == which, ids[0:1], ids[1:2]) - start.astype(f32)
        inside = ((row >= 0.0) & (row < float(tok_count))).astype(f32)
        inside_col = jnp.sum(eye * inside, axis=1, keepdims=True)
        local_col = jnp.sum(eye * row, axis=1, keepdims=True)
        rank = jnp.sum(before * inside_col, axis=0, keepdims=True)
        hit = jnp.where(rank == slot, 1.0, 0.0) * inside
        token_hit = (local_col == iota((cap, tok_count), 1).astype(f32)).astype(f32)
        tables.append(dot(hit, token_hit, 1, 0))
    table = jnp.concatenate(tables, axis=0).astype(bf16)
    second = (iota((2 * GROUP, 1), 0) % GROUP) >= MOST
    for copy in copies[1:]:
        copy.wait()
    rows = jnp.where(second, dot(table, grads[...], 1, 0), dot(table, tokens[...], 1, 0)).astype(bf16)
    own_o[...] = rows[:GROUP]
    other_o[...] = rows[GROUP:]
    number = (iota((SIDE, tok_count), 1) + 1).astype(bf16)
    ids_row = dot(number, table, 1, 1) - 1.0
    kind = (iota((SIDE, 2 * GROUP), 1) % GROUP) >= MOST
    want = iota((SIDE, 2 * GROUP), 0) == 1
    ids_o[...] = jnp.where(kind == want, ids_row, -1.0)


def select(place, picked, tokens, grads):
    width = tokens.shape[1]
    return pl.pallas_call(
        select_body,
        in_specs=[SCALARS] + [ORDER] * 3,
        out_specs=[WHOLE, WHOLE, WHOLE],
        scratch_shapes=[
            pltpu.VMEM(picked.shape, jnp.int32),
            pltpu.VMEM(tokens.shape, bf16),
            pltpu.VMEM(grads.shape, bf16),
            pltpu.SemaphoreType.DMA((1 + 2 * PARTS,)),
        ],
        out_shape=[
            jax.ShapeDtypeStruct((GROUP, width), bf16),
            jax.ShapeDtypeStruct((GROUP, width), bf16),
            jax.ShapeDtypeStruct((SIDE, 2 * GROUP), f32),
        ],
        compiler_params=pltpu.CompilerParams(vmem_limit_bytes=16 * MIB),
        name="select",
    )(place, *in_hbm(picked, tokens, grads))


def expert_body(
    places, counts, near_t, far_t, near_g, far_g, column, shift_h, scale_h, gate_h, up_h, down_h, _,
    hid_o, grows_o, act_o, gpre_o, eo_keep, back_keep, eo_send, back_send, side_o,
    normed_s, eo_s, back_s, weight_s, shift, scale, gate, up, down, vector_sems, up_sems, down_sems,
):
    width = hid_o.shape[1]
    blocks = len(places)
    slots, chunk = up.shape[0], up.shape[2]
    steps = up_h.shape[2] // chunk
    half = blocks // 2

    def fetch(step):
        here = pl.ds(step * chunk, chunk)
        slot = step % slots
        return (
            pltpu.make_async_copy(up_h.at[0, :, here], up.at[slot], up_sems.at[slot]),
            pltpu.make_async_copy(down_h.at[0, here, :], down.at[slot], down_sems.at[slot]),
        )

    vectors = start_copies(((shift_h, shift), (scale_h, scale), (gate_h, gate)), vector_sems)
    fetches = [fetch(step) for step in range(steps)]
    for step in range(min(slots, steps)):
        for copy in fetches[step]:
            copy.start()

    def pair(near, far, block):
        at = MOST * (block % half)
        return (near if block < half else far).at[at : at + GROUP, :]

    for copy in vectors:
        copy.wait()
    one = 1.0 + scale[...]
    place = iota((GROUP, 1), 0)
    for block in range(0, blocks, 2):
        tok = pair(near_t, far_t, block)[...].astype(f32)
        grd = pair(near_g, far_g, places[block])[...].astype(f32)
        rows = pl.ds(block * MOST, GROUP)
        limit = jnp.where(place < MOST, counts[block], counts[block + 1] + MOST)
        filled = (place < limit).astype(f32)
        centered = tok - jnp.mean(tok, axis=1, keepdims=True)
        inverse_std = lax.rsqrt(jnp.mean(centered * centered, axis=1, keepdims=True) + 1e-06)
        normed = centered * inverse_std
        normed_s[rows, :] = normed
        hidden = ((normed * one + shift[...]) * filled).astype(bf16)
        hid_o[rows, :] = hidden
        logit = jnp.sum(hidden.astype(f32) * column[...], axis=1, keepdims=True)
        weight = 1.0 / (1.0 + jnp.exp(-logit))
        weight_s[rows, :] = jnp.broadcast_to(weight, (GROUP, 128))
        grows_o[rows, :] = (weight * (gate[...] * grd)).astype(bf16)

    for step in range(steps):
        slot = step % slots
        for copy in fetches[step]:
            copy.wait()
        up_block, down_block = up[slot], down[slot]
        pre = dot(hid_o[...], up_block, 1, 0)
        grad_act = dot(grows_o[...], down_block, 1, 1)
        square = pre * pre
        tangent = jnp.tanh(GELU_C * (pre + 0.044715 * square * pre))
        act = (0.5 * pre * (1.0 + tangent)).astype(bf16)
        slope = 0.5 * (1.0 + tangent) + 0.5 * pre * (1.0 - tangent * tangent) * GELU_C * (
            1.0 + 3.0 * 0.044715 * square
        )
        grad_pre = (grad_act * slope).astype(bf16)
        here = pl.ds(step * chunk, chunk)
        act_o[:, here] = act
        gpre_o[:, here] = grad_pre
        eo, back = dot(act, down_block, 1, 0), dot(grad_pre, up_block, 1, 1)
        if step == 0:
            eo_s[...] = eo
            back_s[...] = back
        else:
            eo_s[...] += eo
            back_s[...] += back
        if step + slots < steps:
            for copy in fetches[step + slots]:
                copy.start()

    gate_v = shift_v = scale_v = router_v = jnp.zeros((1, width), f32)
    for block in range(0, blocks, 2):
        grd = pair(near_g, far_g, places[block])[...].astype(f32)
        rows = pl.ds(block * MOST, GROUP)
        weight = weight_s[rows, 0:1]
        eo = eo_s[rows, :]
        grad_logit = jnp.sum(gate[...] * grd * eo, axis=1, keepdims=True) * weight * (1.0 - weight)
        eo = weight * eo
        back = back_s[rows, :] + grad_logit * column[...]
        gate_v += jnp.sum(grd * eo, axis=0, keepdims=True)
        shift_v += jnp.sum(back, axis=0, keepdims=True)
        scale_v += jnp.sum(back * normed_s[rows, :], axis=0, keepdims=True)
        router_v += jnp.sum(grad_logit * hid_o[rows, :].astype(f32), axis=0, keepdims=True)
        for values, keep, send, at in ((eo, eo_keep, eo_send, block), (back, back_keep, back_send, places[block])):
            if at < half:
                pair(keep, None, at)[...] = values
            else:
                pair(None, send, at)[...] = values.astype(bf16)
    side = jnp.concatenate([gate_v, shift_v, scale_v, router_v, jnp.zeros((SIDE - 4, width), f32)], axis=0)
    side_o[...] = side
    eo_send[MOST * half :, :] = jnp.concatenate([side, jnp.zeros_like(side)], axis=0).astype(bf16)


def experts(places, counts, near_t, far_t, near_g, far_g, shift, scale, gate, column, up, down, behind):
    blocks = counts.shape[0]
    slot_count = blocks * MOST
    width, hid_count = up.shape[1], up.shape[2]
    chunk = min(256, hid_count)
    buffers = min(3, hid_count // chunk)
    rows = MOST * blocks // 2
    return pl.pallas_call(
        functools.partial(expert_body, places),
        in_specs=[SCALARS] + [WHOLE] * 5 + [ORDER] * 6,
        out_specs=[WHOLE] * 9,
        out_shape=[
            jax.ShapeDtypeStruct((slot_count, width), bf16),
            jax.ShapeDtypeStruct((slot_count, width), bf16),
            jax.ShapeDtypeStruct((slot_count, hid_count), bf16),
            jax.ShapeDtypeStruct((slot_count, hid_count), bf16),
            jax.ShapeDtypeStruct((rows, width), f32),
            jax.ShapeDtypeStruct((rows, width), f32),
            jax.ShapeDtypeStruct((rows + GROUP, width), bf16),
            jax.ShapeDtypeStruct((rows, width), bf16),
            jax.ShapeDtypeStruct((SIDE, width), f32),
        ],
        scratch_shapes=[pltpu.VMEM((slot_count, width), f32)] * 3
        + [pltpu.VMEM((slot_count, 128), f32)]
        + [pltpu.VMEM((1, width), f32)] * 3
        + [pltpu.VMEM((buffers, width, chunk), bf16), pltpu.VMEM((buffers, chunk, width), bf16)]
        + [pltpu.SemaphoreType.DMA((n,)) for n in (3, buffers, buffers)],
        compiler_params=pltpu.CompilerParams(vmem_limit_bytes=36 * MIB),
        cost_estimate=pl.CostEstimate(
            flops=8 * slot_count * width * hid_count, bytes_accessed=4 * width * hid_count, transcendentals=0
        ),
        name="experts",
    )(counts, near_t, far_t, near_g, far_g, column, *in_hbm(shift, scale, gate, up, down), behind)


def outer_body(left, right, *refs):
    out, done = refs[-2:]
    out[0] = dot(left[...], right[...], 0, 0).astype(bf16)
    done[...] = jnp.zeros_like(done)


def outer(left, right, behind, name, first, count, into=None):
    depth, rows = left.shape
    columns = right.shape[1]
    step = min(rows // 4, 2 * MIB // columns)
    each = rows // 4 // step
    before = [] if into is None else [into]
    return pl.pallas_call(
        outer_body,
        grid=(count * each,),
        in_specs=[pl.BlockSpec((depth, step), lambda i: (0, i + first * each)), WHOLE]
        + [ORDER] * (1 + len(before)),
        out_specs=[pl.BlockSpec((1, step, columns), lambda i: (0, i + first * each, 0)), WHOLE],
        out_shape=[jax.ShapeDtypeStruct((1, rows, columns), bf16), jax.ShapeDtypeStruct((8, 128), f32)],
        input_output_aliases={3: 0} if before else {},
        compiler_params=pltpu.CompilerParams(vmem_limit_bytes=24 * MIB),
        cost_estimate=pl.CostEstimate(
            flops=2 * depth * rows * columns * count, bytes_accessed=rows * columns * count, transcendentals=0
        ),
        name=name,
    )(left, right, behind, *before)


def fold_body(last, keep_e, keep_b, got_e, got_b, side, _, *outs):
    rows = keep_e.shape[0]
    got = got_e[...].astype(f32)
    eo = keep_e[...] + got[:rows]
    back = keep_b[...] + got_b[...].astype(f32)
    total = side[...] + got[rows:]
    outs[0][...] = total
    low, high = slice(0, rows // 2), slice(rows // 2, rows)
    if last:
        outs[1][...] = jnp.concatenate([eo[low], back[low]], axis=0)
        outs[2][...] = jnp.concatenate([eo[high], back[high], total], axis=0).astype(bf16)
    else:
        outs[1][...] = eo[low]
        outs[2][...] = back[low]
        outs[3][...] = jnp.concatenate([eo[high], total], axis=0).astype(bf16)
        outs[4][...] = back[high].astype(bf16)


def fold(keep, got, side, behind):
    rows, width = keep[0].shape
    last = rows == 2 * MOST
    sizes = [(SIDE, f32)]
    if last:
        sizes += [(rows, f32), (rows + SIDE, bf16)]
    else:
        sizes += [(rows // 2, f32)] * 2 + [(rows // 2 + SIDE, bf16), (rows // 2, bf16)]
    return pl.pallas_call(
        functools.partial(fold_body, last),
        in_specs=[WHOLE] * 5 + [ORDER],
        out_specs=[WHOLE] * len(sizes),
        out_shape=[jax.ShapeDtypeStruct((size, width), kind) for size, kind in sizes],
        compiler_params=pltpu.CompilerParams(vmem_limit_bytes=16 * MIB),
        name="fold",
    )(*keep, *got, side, behind)


def pack_body(keep, got, side, ids, _, mine_o):
    theirs = got[...].astype(f32)
    width = theirs.shape[1]
    total = side[...] + theirs[GROUP:]
    numbers = jnp.concatenate([ids[0:2], jnp.full((2, width - ids.shape[1]), -1.0, f32)], axis=1)
    mine_o[...] = jnp.concatenate(
        [keep[...], theirs[:GROUP], total[0:3], numbers, jnp.zeros((SIDE - 5, width), f32)], axis=0
    ).astype(bf16)


def pack(keep, got, side, ids, behind):
    width = keep.shape[1]
    return pl.pallas_call(
        pack_body,
        in_specs=[WHOLE] * 4 + [ORDER],
        out_specs=WHOLE,
        out_shape=jax.ShapeDtypeStruct((2 * GROUP + SIDE, width), bf16),
        compiler_params=pltpu.CompilerParams(vmem_limit_bytes=16 * MIB),
        name="pack",
    )(keep, got, side, ids, behind)


def relay_body(rows, _, rows_o):
    rows_o[...] = rows[...]


def relay(rows, behind):
    return pl.pallas_call(
        relay_body,
        in_specs=[WHOLE, ORDER],
        out_specs=WHOLE,
        out_shape=jax.ShapeDtypeStruct(rows.shape, rows.dtype),
        compiler_params=pltpu.CompilerParams(vmem_limit_bytes=16 * MIB),
        name="relay",
    )(rows, behind)


def normalize_body(tokens, normed_o, inverse_o):
    inputs = tokens[...].astype(f32)
    centered = inputs - jnp.mean(inputs, axis=1, keepdims=True)
    inverse_std = lax.rsqrt(jnp.mean(centered * centered, axis=1, keepdims=True) + 1e-06)
    normed_o[...] = centered * inverse_std
    inverse_o[...] = jnp.broadcast_to(inverse_std, inverse_o.shape)


def normalize(tokens):
    tok_count, width = tokens.shape
    step = min(tok_count, 16)
    return pl.pallas_call(
        normalize_body,
        grid=(tok_count // step,),
        in_specs=[pl.BlockSpec((step, width), lambda i: (i, 0))],
        out_specs=[pl.BlockSpec((step, width), lambda i: (i, 0)), pl.BlockSpec((step, 128), lambda i: (i, 0))],
        out_shape=[jax.ShapeDtypeStruct((tok_count, width), f32), jax.ShapeDtypeStruct((tok_count, 128), f32)],
        compiler_params=pltpu.CompilerParams(vmem_limit_bytes=16 * MIB),
        cost_estimate=pl.CostEstimate(flops=10 * tok_count * width, bytes_accessed=6 * tok_count * width, transcendentals=0),
        name="normalize",
    )(tokens)


def finish_body(
    parts, place, side, got, inverse, scale_h, gate_h, tokens_h, grads_h, normed_h, *refs
):
    pieces = refs[:-16]
    block_h, tgrad_h, gate_o, shift_o, scale_o, router_o = refs[-16:-10]
    scale, gate, tokens, grads, normed, block_s, tgrad_s, vector_sems, in_sems, out_sems = refs[-10:]
    total = tokens.shape[0]
    count = total // parts
    cuts = [pl.ds(k * count, count) for k in range(parts)]
    vectors = start_copies(((scale_h, scale), (gate_h, gate)), vector_sems)
    arrays = ((tokens_h, tokens), (grads_h, grads), (normed_h, normed))
    arrivals = [start_copies([(a.at[cut], b.at[cut]) for a, b in arrays], in_sems.at[k]) for k, cut in enumerate(cuts)]

    rows = jnp.concatenate([piece[: 2 * GROUP, :] for piece in pieces], axis=0)
    ids = [piece[2 * GROUP :, : 2 * GROUP].astype(f32) for piece in pieces]
    ids = [jnp.concatenate([each[3 + kind : 4 + kind] for each in ids], axis=1) for kind in range(2)]
    vector = sum(piece[2 * GROUP :, :].astype(f32) for piece in pieces)
    gate_o[...] = vector[0:1]
    shift_o[...] = vector[1:2]
    scale_o[...] = vector[2:3]
    own, other = side[3:4], got[...].astype(f32)[GROUP + 3 : GROUP + 4]
    first = place[1] == 0
    router_o[0:1] = jnp.where(first, own, other)
    router_o[1:2] = jnp.where(first, other, own)
    for copy in vectors:
        copy.wait()
    one = 1.0 + scale[...]
    departures = []
    for k, cut in enumerate(cuts):
        numbers = (iota((count, rows.shape[0]), 0) + k * count).astype(f32)
        table = jnp.concatenate([(numbers == each).astype(f32) for each in ids], axis=0)
        sums = dot(table.astype(bf16), rows, 1, 0)
        for copy in arrivals[k]:
            copy.wait()
        block_s[cut, :] = (tokens[cut, :].astype(f32) + gate[...] * sums[:count]).astype(bf16)
        grad_norm = sums[count:] * one
        center = jnp.mean(grad_norm, axis=1, keepdims=True)
        along = jnp.mean(grad_norm * normed[cut, :], axis=1, keepdims=True)
        tgrad_s[cut, :] = (
            grads[cut, :].astype(f32) + inverse[cut, 0:1] * (grad_norm - center - normed[cut, :] * along)
        ).astype(bf16)
        departures += start_copies(((block_s.at[cut], block_h.at[cut]), (tgrad_s.at[cut], tgrad_h.at[cut])), out_sems.at[k])
    for copy in departures:
        copy.wait()


def finish(place, side, got, pieces, scale, gate, tokens, grads, normed, inverse):
    tok_count, width = tokens.shape
    parts = 4
    vector = jax.ShapeDtypeStruct((1, width), f32)
    return pl.pallas_call(
        functools.partial(finish_body, parts),
        in_specs=[SCALARS] + [WHOLE] * 3 + [ORDER] * 5 + [WHOLE] * len(pieces),
        out_specs=[ORDER, ORDER] + [WHOLE] * 4,
        out_shape=[jax.ShapeDtypeStruct((tok_count, width), bf16)] * 2
        + [vector] * 3
        + [jax.ShapeDtypeStruct((2, width), f32)],
        scratch_shapes=[pltpu.VMEM((1, width), f32)] * 2
        + [pltpu.VMEM((tok_count, width), kind) for kind in (bf16, bf16, f32, bf16, bf16)]
        + [pltpu.SemaphoreType.DMA(shape) for shape in ((2,), (parts, 3), (parts, 2))],
        compiler_params=pltpu.CompilerParams(vmem_limit_bytes=24 * MIB),
        name="finish",
    )(place, side, got, inverse, *in_hbm(scale, gate, tokens, grads), normed, *pieces)


def swap(values, axis, mask):
    size = lax.axis_size(axis)
    return lax.ppermute(values, axis, [(i, i ^ mask) for i in range(size)])


def halvings(size):
    masks = []
    while size > 1:
        size //= 2
        masks.append(size)
    return masks


def per_device(
    tokens, ada_shift, ada_scale, ada_gate, router, expert_up, expert_down, picked_ids, out_grad
):
    tok_count, width = tokens.shape
    ctx_size, exp_size = lax.axis_size("ctx"), lax.axis_size("exp")
    ctx_masks, exp_masks = halvings(ctx_size), halvings(exp_size)
    me = lax.axis_index("ctx")
    group = me // ctx_masks[0]
    picked = picked_ids[0]
    shift, scale, gate = ada_shift[None], ada_scale[None], ada_gate[None]
    place = jnp.stack([me, group]).astype(jnp.int32)
    own, other, ids = select(place, picked_ids, tokens, out_grad)

    orders = ctx_masks[1:], ctx_masks[:0:-1]
    relative = []
    for order in orders:
        blocks = [0]
        for mask in [ctx_masks[0], *order]:
            blocks = blocks + [r ^ mask for r in blocks]
        relative.append(blocks)
    places = [relative[1].index(r) for r in relative[0]]
    sources = me ^ jnp.array(relative[0], jnp.int32)
    own_ids = jnp.where(group == 0, picked[0], picked[1])
    counts = jnp.sum((own_ids // tok_count)[None, :] == sources[:, None], axis=1).astype(jnp.int32)
    columns = router[0].astype(f32).T
    column = jnp.where(group == 0, columns[0:1], columns[1:2])

    normed, inverse = normalize(tokens)
    got = swap(other, "ctx", ctx_masks[0])
    near = [jnp.concatenate([own[cut], got[cut]], axis=0) for cut in (slice(0, MOST), slice(MOST, GROUP))]
    far = [swap(near[k], "ctx", orders[k][0]) for k in range(2)]
    for masks in zip(orders[0][1:], orders[1][1:]):
        near = [jnp.concatenate([near[k], far[k]], axis=0) for k in range(2)]
        far = [swap(near[k], "ctx", masks[k]) for k in range(2)]
    hidden, grad_rows, act, grad_pre, eo_keep, back_keep, eo_send, back_send, side = experts(
        places, counts, near[0], far[0], near[1], far[1], shift, scale, gate, column, expert_up, expert_down, inverse
    )

    rows = eo_keep.shape[0]
    keep, send = [eo_keep, back_keep], [eo_send[: rows + SIDE], back_send]
    behind = side
    for step, masks in enumerate(zip(orders[0][::-1], orders[1][::-1])):
        got = [swap(send[k], "ctx", masks[k]) for k in range(2)]
        if step == 0:
            up_grad, behind = outer(hidden, grad_pre, behind, "up_grad", 0, 3)
        elif step == 1:
            down_grad, behind = outer(act, grad_rows, behind, "down_grad", 0, 2)
        side, *rest = fold(keep, got, side, behind)
        keep, send = rest[:-2], rest[-2:]
        behind = side
    keep, send = rest
    got = swap(send, "ctx", ctx_masks[0])
    down_grad, behind = outer(act, grad_rows, behind, "down_grad", 2, 2, down_grad)
    mine = pack(keep, got, side, ids, behind)
    pieces = [mine]
    for step, mask in enumerate(exp_masks):
        come = [swap(piece, "exp", mask) for piece in pieces]
        if step == 0:
            up_grad, behind = outer(hidden, grad_pre, mine, "up_grad", 3, 1, up_grad)
            come = [relay(piece, behind) for piece in come]
        pieces = pieces + come
    block_out, tokens_grad, gate_grad, shift_grad, scale_grad, router_rows = finish(
        place, side, got, pieces, scale, gate, tokens, out_grad, normed, inverse
    )
    return (
        block_out,
        tokens_grad,
        up_grad,
        down_grad,
        router_rows.T[None],
        shift_grad[0],
        scale_grad[0],
        gate_grad[0],
    )


def solution(mesh):
    in_specs = (
        P("ctx", None),
        P(),
        P(),
        P(),
        P("exp", None, None),
        P("exp", None, "ctx"),
        P("exp", "ctx", None),
        P("exp", None, None),
        P("ctx", None),
    )
    out_specs = (
        P("ctx", None),
        P("ctx", None),
        P("exp", None, "ctx"),
        P("exp", "ctx", None),
        P("exp", None, None),
        P(),
        P(),
        P(),
    )
    return jax.shard_map(
        per_device, mesh=mesh, in_specs=in_specs, out_specs=out_specs, check_vma=False
    )
```

```python
import functools

import jax
import jax.numpy as jnp
from jax import lax
from jax.experimental import pallas as pl
from jax.experimental.pallas import tpu as pltpu
from jax.sharding import PartitionSpec as P

MOST = 8
GROUP = 2 * MOST
PARTS = 4
SIDE = 8
LANES = 128
GELU_C = 0.7978845608028654
MIB = 1 << 20
CHUNK = 256
SHARE = MIB // 2
EARLY = (1, 1, 2)
f32, bf16 = jnp.float32, jnp.bfloat16
WHOLE = pl.BlockSpec(memory_space=pltpu.VMEM)
SCALARS = pl.BlockSpec(memory_space=pltpu.SMEM)
ORDER = pl.BlockSpec(memory_space=pl.ANY)


def in_hbm(*arrays):
    return [pltpu.with_memory_space_constraint(array, pltpu.HBM) for array in arrays]


def fold_vector(row):
    return jnp.concatenate([row[:, k : k + LANES] for k in range(0, row.shape[1], LANES)], axis=0)


def spread(vector, rows):
    depth = vector.shape[0]
    if rows > depth:
        return jnp.concatenate([vector, jnp.zeros((rows - depth, LANES), f32)], axis=0)
    return jnp.concatenate([vector[k : k + rows] for k in range(0, depth, rows)], axis=1)


def spread_columns(width, rows):
    return LANES * max(1, width // LANES // rows)


def unspread(columns, width):
    rows = columns.shape[0]
    depth, each = width // LANES, spread_columns(width, rows)
    vectors = []
    for at in range(0, columns.shape[1], each):
        cuts = [columns[:, k : k + LANES] for k in range(at, at + each, LANES)]
        vectors.append(jnp.concatenate(cuts, axis=0)[:depth])
    return vectors


def start_copies(pairs, sems):
    copies = [pltpu.make_async_copy(a, b, sems.at[k]) for k, (a, b) in enumerate(pairs)]
    for copy in copies:
        copy.start()
    return copies


def dot(left, right, left_dim, right_dim):
    return lax.dot_general(
        left, right, (((left_dim,), (right_dim,)), ((), ())), preferred_element_type=f32
    )


def iota(shape, dim):
    return lax.broadcasted_iota(jnp.int32, shape, dim)


def select_body(place, picked_h, tokens_h, grads_h, own_o, other_o, ids_o, picked, tokens, grads, sems):
    tok_count = tokens.shape[0]
    pairs = [(picked_h, picked)]
    for k in range(PARTS):
        cut = pl.ds(k * (tok_count // PARTS), tok_count // PARTS)
        pairs += [(tokens_h.at[cut], tokens.at[cut]), (grads_h.at[cut], grads.at[cut])]
    copies = start_copies(pairs, sems)
    cap = picked.shape[2]
    start = place[0] * tok_count
    group = place[1]
    copies[0].wait()
    ids = picked[0].astype(f32)
    lanes, rows = iota((cap, cap), 1), iota((cap, cap), 0)
    eye = (lanes == rows).astype(f32)
    before = (rows < lanes).astype(f32)
    slot = (iota((GROUP, cap), 0) % MOST).astype(f32)
    tables = []
    for which in range(2):
        row = jnp.where(group == which, ids[0:1], ids[1:2]) - start.astype(f32)
        inside = ((row >= 0.0) & (row < float(tok_count))).astype(f32)
        inside_col = jnp.sum(eye * inside, axis=1, keepdims=True)
        local_col = jnp.sum(eye * row, axis=1, keepdims=True)
        rank = jnp.sum(before * inside_col, axis=0, keepdims=True)
        hit = jnp.where(rank == slot, 1.0, 0.0) * inside
        token_hit = (local_col == iota((cap, tok_count), 1).astype(f32)).astype(f32)
        tables.append(dot(hit, token_hit, 1, 0))
    table = jnp.concatenate(tables, axis=0).astype(bf16)
    second = (iota((2 * GROUP, 1), 0) % GROUP) >= MOST
    for copy in copies[1:]:
        copy.wait()
    rows = jnp.where(second, dot(table, grads[...], 1, 0), dot(table, tokens[...], 1, 0)).astype(bf16)
    own_o[...] = rows[:GROUP]
    other_o[...] = rows[GROUP:]
    number = (iota((SIDE, tok_count), 1) + 1).astype(bf16)
    ids_row = dot(number, table, 1, 1) - 1.0
    kind = (iota((SIDE, 2 * GROUP), 1) % GROUP) >= MOST
    want = iota((SIDE, 2 * GROUP), 0) == 1
    ids_o[...] = jnp.where(kind == want, ids_row, -1.0)


def select(place, picked, tokens, grads):
    width = tokens.shape[1]
    return pl.pallas_call(
        select_body,
        in_specs=[SCALARS] + [ORDER] * 3,
        out_specs=[WHOLE, WHOLE, WHOLE],
        scratch_shapes=[
            pltpu.VMEM(picked.shape, jnp.int32),
            pltpu.VMEM(tokens.shape, bf16),
            pltpu.VMEM(grads.shape, bf16),
            pltpu.SemaphoreType.DMA((1 + 2 * PARTS,)),
        ],
        out_shape=[
            jax.ShapeDtypeStruct((GROUP, width), bf16),
            jax.ShapeDtypeStruct((GROUP, width), bf16),
            jax.ShapeDtypeStruct((SIDE, 2 * GROUP), f32),
        ],
        compiler_params=pltpu.CompilerParams(vmem_limit_bytes=16 * MIB),
        name="select",
    )(place, *in_hbm(picked, tokens, grads))


def fetch(up_h, down_h, up, down, sems, first, count):
    pairs = []
    for k in range(count):
        here = pl.ds((first + k) * CHUNK, CHUNK)
        pairs += [(up_h.at[0, :, here], up.at[k]), (down_h.at[0, here, :], down.at[k])]
    return start_copies(pairs, sems)


def bring_body(first, up_h, down_h, _, up_o, down_o, done, sems):
    copies = fetch(up_h, down_h, up_o, down_o, sems, first, up_o.shape[0])
    done[...] = jnp.zeros_like(done)
    for copy in copies:
        copy.wait()


def bring(up, down, behind, first, count):
    width = up.shape[1]
    return pl.pallas_call(
        functools.partial(bring_body, first),
        in_specs=[ORDER] * 3,
        out_specs=[WHOLE] * 3,
        out_shape=[
            pltpu.VMEM((count, width, CHUNK), bf16),
            pltpu.VMEM((count, CHUNK, width), bf16),
            jax.ShapeDtypeStruct((8, 128), f32),
        ],
        scratch_shapes=[pltpu.SemaphoreType.DMA((2 * count,))],
        compiler_params=pltpu.CompilerParams(vmem_limit_bytes=8 * MIB),
        cost_estimate=pl.CostEstimate(flops=0, bytes_accessed=4 * count * width * CHUNK, transcendentals=0),
        name="bring",
    )(*in_hbm(up, down), behind)


def join_body(first, near_t, near_g, far_t, far_g, _, tokens_o, grads_o):
    if first:
        rows = [ref[...].astype(f32) for ref in (near_t, far_t)]
        tokens_o[...] = jnp.concatenate([r[:MOST] for r in rows], axis=0).astype(bf16)
        grads_o[...] = jnp.concatenate([r[MOST:] for r in rows], axis=0).astype(bf16)
    else:
        tokens_o[...] = jnp.concatenate([near_t[...], far_t[...]], axis=0)
        grads_o[...] = jnp.concatenate([near_g[...], far_g[...]], axis=0)


def join(first, near, far, behind):
    rows, width = near[0].shape
    rows = rows if first else 2 * rows
    return pl.pallas_call(
        functools.partial(join_body, first),
        in_specs=[WHOLE] * 4 + [ORDER],
        out_specs=[WHOLE] * 2,
        out_shape=[jax.ShapeDtypeStruct((rows, width), bf16)] * 2,
        compiler_params=pltpu.CompilerParams(vmem_limit_bytes=8 * MIB),
        name="join",
    )(*near, *far, behind)


def expert_body(
    places, counts, near_t, far_t, near_g, far_g, column, shift, one, gate, up_h, down_h, *refs
):
    early, refs = refs[:-16], refs[-16:]
    hid_o, grows_o, act_o, gpre_o, eo_keep, back_keep, eo_send, back_send, side_o = refs[:9]
    normed_s, eo_s, back_s, weight_s, up_s, down_s, sems = refs[9:]
    width = hid_o.shape[1]
    blocks = len(places)
    half = blocks // 2
    chunk = up_s.shape[2]
    at_hand = [(up.at[k], down.at[k]) for up, down in zip(early[::2], early[1::2]) for k in range(up.shape[0])]
    steps = up_h.shape[2] // chunk
    late = fetch(up_h, down_h, up_s, down_s, sems, len(at_hand), steps - len(at_hand))

    def pair(near, far, block):
        at = MOST * (block % half)
        return (near if block < half else far).at[at : at + GROUP, :]

    place = iota((GROUP, 1), 0)
    for block in range(0, blocks, 2):
        tok = pair(near_t, far_t, block)[...].astype(f32)
        grd = pair(near_g, far_g, places[block])[...].astype(f32)
        rows = pl.ds(block * MOST, GROUP)
        limit = jnp.where(place < MOST, counts[block], counts[block + 1] + MOST)
        filled = (place < limit).astype(f32)
        centered = tok - jnp.mean(tok, axis=1, keepdims=True)
        inverse_std = lax.rsqrt(jnp.mean(centered * centered, axis=1, keepdims=True) + 1e-06)
        normed = centered * inverse_std
        normed_s[rows, :] = normed
        hidden = ((normed * one[...] + shift[...]) * filled).astype(bf16)
        hid_o[rows, :] = hidden
        logit = jnp.sum(hidden.astype(f32) * column[...], axis=1, keepdims=True)
        weight = 1.0 / (1.0 + jnp.exp(-logit))
        weight_s[rows, :] = jnp.broadcast_to(weight, (GROUP, 128))
        grows_o[rows, :] = (weight * (gate[...] * grd)).astype(bf16)

    for step in range(steps):
        here = pl.ds(step * chunk, chunk)
        if step < len(at_hand):
            up_block, down_block = [ref[...] for ref in at_hand[step]]
        else:
            k = step - len(at_hand)
            late[2 * k].wait()
            late[2 * k + 1].wait()
            up_block, down_block = up_s[k], down_s[k]
        pre = dot(hid_o[...], up_block, 1, 0)
        grad_act = dot(grows_o[...], down_block, 1, 1)
        square = pre * pre
        tangent = jnp.tanh(GELU_C * (pre + 0.044715 * square * pre))
        act = (0.5 * pre * (1.0 + tangent)).astype(bf16)
        slope = 0.5 * (1.0 + tangent) + 0.5 * pre * (1.0 - tangent * tangent) * GELU_C * (
            1.0 + 3.0 * 0.044715 * square
        )
        grad_pre = (grad_act * slope).astype(bf16)
        act_o[:, here] = act
        gpre_o[:, here] = grad_pre
        eo, back = dot(act, down_block, 1, 0), dot(grad_pre, up_block, 1, 1)
        if step == 0:
            eo_s[...] = eo
            back_s[...] = back
        else:
            eo_s[...] += eo
            back_s[...] += back

    gate_v = shift_v = scale_v = router_v = jnp.zeros((1, width), f32)
    for block in range(0, blocks, 2):
        grd = pair(near_g, far_g, places[block])[...].astype(f32)
        rows = pl.ds(block * MOST, GROUP)
        weight = weight_s[rows, 0:1]
        eo = eo_s[rows, :]
        grad_logit = jnp.sum(gate[...] * grd * eo, axis=1, keepdims=True) * weight * (1.0 - weight)
        eo = weight * eo
        back = back_s[rows, :] + grad_logit * column[...]
        gate_v += jnp.sum(grd * eo, axis=0, keepdims=True)
        shift_v += jnp.sum(back, axis=0, keepdims=True)
        scale_v += jnp.sum(back * normed_s[rows, :], axis=0, keepdims=True)
        router_v += jnp.sum(grad_logit * hid_o[rows, :].astype(f32), axis=0, keepdims=True)
        for values, keep, send, at in ((eo, eo_keep, eo_send, block), (back, back_keep, back_send, places[block])):
            if at < half:
                pair(keep, None, at)[...] = values
            else:
                here = MOST * (at % half)
                send[here : here + GROUP, :width] = values.astype(bf16)
    sums = [fold_vector(row) for row in (gate_v, shift_v, scale_v, router_v)]
    side_o[...] = jnp.concatenate(sums, axis=0)
    rows = eo_send.shape[0]
    eo_send[:, width:] = jnp.concatenate([spread(v, rows) for v in sums[:2]], axis=1).astype(bf16)
    back_send[:, width:] = jnp.concatenate([spread(v, rows) for v in sums[2:]], axis=1).astype(bf16)


def experts(places, counts, near_t, far_t, near_g, far_g, shift, one, gate, column, up, down, early):
    blocks = counts.shape[0]
    slot_count = blocks * MOST
    width, hid_count = up.shape[1], up.shape[2]
    late = max(1, hid_count // CHUNK - sum(part.shape[0] for part in early[::2]))
    rows = MOST * blocks // 2
    return pl.pallas_call(
        functools.partial(expert_body, places),
        in_specs=[SCALARS] + [WHOLE] * 8 + [ORDER] * 2 + [WHOLE] * len(early),
        out_specs=[WHOLE] * 9,
        out_shape=[
            jax.ShapeDtypeStruct((slot_count, width), bf16),
            jax.ShapeDtypeStruct((slot_count, width), bf16),
            jax.ShapeDtypeStruct((slot_count, hid_count), bf16),
            jax.ShapeDtypeStruct((slot_count, hid_count), bf16),
            jax.ShapeDtypeStruct((rows, width), f32),
            jax.ShapeDtypeStruct((rows, width), f32),
            jax.ShapeDtypeStruct((rows, width + 2 * spread_columns(width, rows)), bf16),
            jax.ShapeDtypeStruct((rows, width + 2 * spread_columns(width, rows)), bf16),
            jax.ShapeDtypeStruct((4 * width // LANES, LANES), f32),
        ],
        scratch_shapes=[pltpu.VMEM((slot_count, width), f32)] * 3
        + [pltpu.VMEM((slot_count, 128), f32)]
        + [pltpu.VMEM((late, width, CHUNK), bf16), pltpu.VMEM((late, CHUNK, width), bf16)]
        + [pltpu.SemaphoreType.DMA((2 * late,))],
        compiler_params=pltpu.CompilerParams(vmem_limit_bytes=(12 * max(1, slot_count // 64) + 4 * late) * MIB),
        cost_estimate=pl.CostEstimate(
            flops=8 * slot_count * width * hid_count, bytes_accessed=4 * width * hid_count, transcendentals=0
        ),
        name="experts",
    )(counts, near_t, far_t, near_g, far_g, column, shift, one, gate, *in_hbm(up, down), *early)


def outer_body(step, left, right, *refs):
    out_h, done, out, sems = refs[-4:]
    done[...] = jnp.zeros_like(done)
    first = refs[-5]
    copies = []
    for k in range(out.shape[0] // step):
        here = pl.ds(k * step, step)
        out[here, :] = dot(left[:, first + k * step : first + (k + 1) * step], right[...], 0, 0).astype(bf16)
        copies += start_copies([(out.at[here], out_h.at[0, pl.ds(first + k * step, step)])], sems.at[pl.ds(k, 1)])
    for copy in copies:
        copy.wait()


def outer(left, right, behind, name, first, count, into=None):
    depth, rows = left.shape
    columns = right.shape[1]
    share = count * rows // 4
    step = min(rows // 4, SHARE // columns)
    before = [] if into is None else [into]

    def body(left, right, _, *refs):
        outer_body(step, left, right, first * rows // 4, *refs[-4:])

    return pl.pallas_call(
        body,
        in_specs=[WHOLE] * 2 + [ORDER] * (1 + len(before)),
        out_specs=[ORDER, WHOLE],
        out_shape=[jax.ShapeDtypeStruct((1, rows, columns), bf16), jax.ShapeDtypeStruct((8, 128), f32)],
        scratch_shapes=[pltpu.VMEM((share, columns), bf16), pltpu.SemaphoreType.DMA((share // step,))],
        input_output_aliases={3: 0} if before else {},
        compiler_params=pltpu.CompilerParams(vmem_limit_bytes=24 * MIB),
        cost_estimate=pl.CostEstimate(
            flops=2 * depth * rows * columns * count, bytes_accessed=rows * columns * count, transcendentals=0
        ),
        name=name,
    )(left, right, behind, *before)


def fold_body(last, keep_e, keep_b, got_e, got_b, side, _, *outs):
    rows, width = keep_e.shape
    depth = width // LANES
    got = [got_e[...].astype(f32), got_b[...].astype(f32)]
    eo = keep_e[...] + got[0][:, :width]
    back = keep_b[...] + got[1][:, :width]
    theirs = unspread(got[0][:, width:], width) + unspread(got[1][:, width:], width)
    sums = [side[k * depth : (k + 1) * depth] + v for k, v in enumerate(theirs)]
    outs[0][...] = jnp.concatenate(sums, axis=0)
    low, high = slice(0, rows // 2), slice(rows // 2, rows)
    if last:
        outs[1][...] = jnp.concatenate([eo[low], back[low]], axis=0)
        send = jnp.concatenate([eo[high], back[high]], axis=0)
        outs[2][...] = jnp.concatenate([send] + [spread(v, rows) for v in sums], axis=1).astype(bf16)
    else:
        outs[1][...] = eo[low]
        outs[2][...] = back[low]
        outs[3][...] = jnp.concatenate([eo[high]] + [spread(v, rows // 2) for v in sums[:2]], axis=1).astype(bf16)
        outs[4][...] = jnp.concatenate([back[high]] + [spread(v, rows // 2) for v in sums[2:]], axis=1).astype(bf16)


def fold(keep, got, side, behind):
    rows, width = keep[0].shape
    last = rows == 2 * MOST
    shapes = [(side.shape, f32)]
    if last:
        shapes += [((rows, width), f32), ((rows, width + 4 * spread_columns(width, rows)), bf16)]
    else:
        wide = width + 2 * spread_columns(width, rows // 2)
        shapes += [((rows // 2, width), f32)] * 2 + [((rows // 2, wide), bf16)] * 2
    return pl.pallas_call(
        functools.partial(fold_body, last),
        in_specs=[WHOLE] * 5 + [ORDER],
        out_specs=[WHOLE] * len(shapes),
        out_shape=[jax.ShapeDtypeStruct(shape, kind) for shape, kind in shapes],
        compiler_params=pltpu.CompilerParams(vmem_limit_bytes=16 * MIB),
        name="fold",
    )(*keep, *got, side, behind)


def pack_body(keep, got, side, ids, _, mine_o):
    width = keep.shape[1]
    depth = width // LANES
    theirs = got[...].astype(f32)
    sums = [side[k * depth : (k + 1) * depth] + v for k, v in enumerate(unspread(theirs[:, width:], width)[:3])]
    rows = mine_o.shape[0]
    numbers = jnp.concatenate([ids[...], jnp.full((SIDE, LANES - ids.shape[1]), -1.0, f32)], axis=1)
    numbers = jnp.concatenate([numbers, jnp.zeros((rows - SIDE, LANES), f32)], axis=0)
    mine = jnp.concatenate([keep[...], theirs[:, :width]], axis=0)
    mine_o[...] = jnp.concatenate([mine] + [spread(v, rows) for v in sums] + [numbers], axis=1).astype(bf16)


def pack(keep, got, side, ids, behind):
    width = keep.shape[1]
    rows = 2 * GROUP
    return pl.pallas_call(
        pack_body,
        in_specs=[WHOLE] * 4 + [ORDER],
        out_specs=WHOLE,
        out_shape=jax.ShapeDtypeStruct((rows, width + 3 * spread_columns(width, rows) + LANES), bf16),
        compiler_params=pltpu.CompilerParams(vmem_limit_bytes=16 * MIB),
        name="pack",
    )(keep, got, side, ids, behind)


def relay_body(rows, _, rows_o):
    rows_o[...] = rows[...]


def relay(rows, behind):
    return pl.pallas_call(
        relay_body,
        in_specs=[WHOLE, ORDER],
        out_specs=WHOLE,
        out_shape=jax.ShapeDtypeStruct(rows.shape, rows.dtype),
        compiler_params=pltpu.CompilerParams(vmem_limit_bytes=16 * MIB),
        name="relay",
    )(rows, behind)


def normalize_body(tokens, grads, shift, scale, gate, normed_o, inverse_o, tokens_o, grads_o, shift_o, one_o, gate_o):
    inputs = tokens[...].astype(f32)
    centered = inputs - jnp.mean(inputs, axis=1, keepdims=True)
    inverse_std = lax.rsqrt(jnp.mean(centered * centered, axis=1, keepdims=True) + 1e-06)
    normed_o[...] = centered * inverse_std
    inverse_o[...] = jnp.broadcast_to(inverse_std, inverse_o.shape)
    tokens_o[...] = tokens[...]
    grads_o[...] = grads[...]
    shift_o[...] = shift[...]
    one_o[...] = 1.0 + scale[...]
    gate_o[...] = gate[...]


def normalize(tokens, grads, shift, scale, gate):
    tok_count, width = tokens.shape
    step = min(tok_count, 32)
    wide = pl.BlockSpec((step, width), lambda i: (i, 0))
    narrow = pl.BlockSpec((step, 128), lambda i: (i, 0))
    line = pl.BlockSpec((1, width), lambda i: (0, 0))
    return pl.pallas_call(
        normalize_body,
        grid=(tok_count // step,),
        in_specs=[wide, wide, line, line, line],
        out_specs=[wide, narrow, wide, wide, line, line, line],
        out_shape=[
            jax.ShapeDtypeStruct((tok_count, width), f32),
            jax.ShapeDtypeStruct((tok_count, 128), f32),
            jax.ShapeDtypeStruct((tok_count, width), bf16),
            jax.ShapeDtypeStruct((tok_count, width), bf16),
        ]
        + [jax.ShapeDtypeStruct((1, width), f32)] * 3,
        compiler_params=pltpu.CompilerParams(vmem_limit_bytes=16 * MIB),
        cost_estimate=pl.CostEstimate(flops=10 * tok_count * width, bytes_accessed=6 * tok_count * width, transcendentals=0),
        name="normalize",
    )(*in_hbm(tokens, grads, shift, scale, gate))


def finish_body(
    parts, place, side, got, inverse, tokens, grads, normed, one, gate, *refs
):
    pieces = refs[:-14]
    block_h, tgrad_h, gate_h, shift_h, scale_h, router_h = refs[-14:-8]
    gate_s, shift_s, scale_s, router_s, block_s, tgrad_s, vector_sems, out_sems = refs[-8:]
    total = tokens.shape[0]
    count = total // parts
    cuts = [pl.ds(k * count, count) for k in range(parts)]
    width = tokens.shape[1]
    depth = width // LANES
    rows = jnp.concatenate([piece[:, :width] for piece in pieces], axis=0)
    ids = [piece[:, piece.shape[1] - LANES :].astype(f32)[:, : 2 * GROUP] for piece in pieces]
    ids = [jnp.concatenate([each[kind : 1 + kind] for each in ids], axis=1) for kind in range(2)]
    vector = sum(piece[:, width : piece.shape[1] - LANES].astype(f32) for piece in pieces)
    gate_s[...], shift_s[...], scale_s[...] = unspread(vector, width)
    own = side[3 * depth :]
    other = unspread(got[...].astype(f32)[:, width:], width)[3]
    first = place[1] == 0
    for k, row in enumerate((jnp.where(first, own, other), jnp.where(first, other, own))):
        router_s[k : k + 1] = jnp.concatenate([row[at : at + 1] for at in range(depth)], axis=1)
    departures = start_copies(
        ((gate_s, gate_h), (shift_s, shift_h), (scale_s, scale_h), (router_s, router_h)), vector_sems
    )
    for k, cut in enumerate(cuts):
        numbers = (iota((count, rows.shape[0]), 0) + k * count).astype(f32)
        table = jnp.concatenate([(numbers == each).astype(f32) for each in ids], axis=0)
        sums = dot(table.astype(bf16), rows, 1, 0)
        block_s[cut, :] = (tokens[cut, :].astype(f32) + gate[...] * sums[:count]).astype(bf16)
        grad_norm = sums[count:] * one[...]
        center = jnp.mean(grad_norm, axis=1, keepdims=True)
        along = jnp.mean(grad_norm * normed[cut, :], axis=1, keepdims=True)
        tgrad_s[cut, :] = (
            grads[cut, :].astype(f32) + inverse[cut, 0:1] * (grad_norm - center - normed[cut, :] * along)
        ).astype(bf16)
        departures += start_copies(((block_s.at[cut], block_h.at[cut]), (tgrad_s.at[cut], tgrad_h.at[cut])), out_sems.at[k])
    for copy in departures:
        copy.wait()


def finish(place, side, got, pieces, one, gate, tokens, grads, normed, inverse):
    tok_count, width = tokens.shape
    parts = 4
    vector = jax.ShapeDtypeStruct((width // LANES, LANES), f32)
    return pl.pallas_call(
        functools.partial(finish_body, parts),
        in_specs=[SCALARS] + [WHOLE] * (8 + len(pieces)),
        out_specs=[ORDER] * 6,
        out_shape=[jax.ShapeDtypeStruct((tok_count, width), bf16)] * 2
        + [vector] * 3
        + [jax.ShapeDtypeStruct((2, width), f32)],
        scratch_shapes=[pltpu.VMEM(vector.shape, f32)] * 3
        + [pltpu.VMEM((2, width), f32)]
        + [pltpu.VMEM((tok_count, width), kind) for kind in (bf16, bf16)]
        + [pltpu.SemaphoreType.DMA(shape) for shape in ((4,), (parts, 2))],
        compiler_params=pltpu.CompilerParams(vmem_limit_bytes=24 * MIB),
        name="finish",
    )(place, side, got, inverse, tokens, grads, normed, one, gate, *pieces)


def swap(values, axis, mask):
    size = lax.axis_size(axis)
    return lax.ppermute(values, axis, [(i, i ^ mask) for i in range(size)])


def halvings(size):
    masks = []
    while size > 1:
        size //= 2
        masks.append(size)
    return masks


def per_device(
    tokens, ada_shift, ada_scale, ada_gate, router, expert_up, expert_down, picked_ids, out_grad
):
    tok_count, width = tokens.shape
    ctx_size, exp_size = lax.axis_size("ctx"), lax.axis_size("exp")
    ctx_masks, exp_masks = halvings(ctx_size), halvings(exp_size)
    me = lax.axis_index("ctx")
    group = me // ctx_masks[0]
    picked = picked_ids[0]
    shift, scale, gate = ada_shift[None], ada_scale[None], ada_gate[None]
    place = jnp.stack([me, group]).astype(jnp.int32)
    own, other, ids = select(place, picked_ids, tokens, out_grad)

    orders = ctx_masks[1:], ctx_masks[:0:-1]
    relative = []
    for order in orders:
        blocks = [0]
        for mask in [ctx_masks[0], *order]:
            blocks = blocks + [r ^ mask for r in blocks]
        relative.append(blocks)
    places = [relative[1].index(r) for r in relative[0]]
    sources = me ^ jnp.array(relative[0], jnp.int32)
    own_ids = jnp.where(group == 0, picked[0], picked[1])
    counts = jnp.sum((own_ids // tok_count)[None, :] == sources[:, None], axis=1).astype(jnp.int32)
    columns = router[0].astype(f32).T
    column = jnp.where(group == 0, columns[0:1], columns[1:2])

    normed, inverse, near_tokens, near_grads, shift, one, gate = normalize(tokens, out_grad, shift, scale, gate)
    early, brought, behind = [], 0, own

    def bring_some(step):
        nonlocal brought, behind
        count = min(EARLY[step] if step < len(EARLY) else 0, expert_up.shape[2] // CHUNK - brought)
        if count > 0:
            *weights, behind = bring(expert_up, expert_down, behind, brought, count)
            early.extend(weights)
            brought += count

    got = swap(other, "ctx", ctx_masks[0])
    bring_some(0)
    near = join(True, [own, own], [got, got], behind)
    far = [swap(near[k], "ctx", orders[k][0]) for k in range(2)]
    for step, masks in enumerate(zip(orders[0][1:], orders[1][1:])):
        behind = near[0]
        bring_some(1 + step)
        near = join(False, near, far, behind)
        far = [swap(near[k], "ctx", masks[k]) for k in range(2)]
    behind = near[0]
    bring_some(len(orders[0]))
    hidden, grad_rows, act, grad_pre, eo_keep, back_keep, eo_send, back_send, side = experts(
        places, counts, near[0], far[0], near[1], far[1], shift, one, gate, column, expert_up, expert_down, early
    )

    rows = eo_keep.shape[0]
    keep, send = [eo_keep, back_keep], [eo_send, back_send]
    behind = side
    for step, masks in enumerate(zip(orders[0][::-1], orders[1][::-1])):
        got = [swap(send[k], "ctx", masks[k]) for k in range(2)]
        if step == 0:
            up_grad, behind = outer(hidden, grad_pre, behind, "up_grad", 0, 3)
        elif step == 1:
            down_grad, behind = outer(act, grad_rows, behind, "down_grad", 0, 2)
        side, *rest = fold(keep, got, side, behind)
        keep, send = rest[:-2], rest[-2:]
        behind = side
    keep, send = rest
    got = swap(send, "ctx", ctx_masks[0])
    down_grad, behind = outer(act, grad_rows, behind, "down_grad", 2, 2, down_grad)
    mine = pack(keep, got, side, ids, behind)
    pieces = [mine]
    for step, mask in enumerate(exp_masks):
        come = [swap(piece, "exp", mask) for piece in pieces]
        if step == 0:
            up_grad, behind = outer(hidden, grad_pre, mine, "up_grad", 3, 1, up_grad)
            come = [relay(piece, behind) for piece in come]
        pieces = pieces + come
    block_out, tokens_grad, gate_grad, shift_grad, scale_grad, router_rows = finish(
        place, side, got, pieces, one, gate, near_tokens, near_grads, normed, inverse
    )
    return (
        block_out,
        tokens_grad,
        up_grad,
        down_grad,
        router_rows.T[None],
        shift_grad.reshape(width),
        scale_grad.reshape(width),
        gate_grad.reshape(width),
    )


def solution(mesh):
    in_specs = (
        P("ctx", None),
        P(),
        P(),
        P(),
        P("exp", None, None),
        P("exp", None, "ctx"),
        P("exp", "ctx", None),
        P("exp", None, None),
        P("ctx", None),
    )
    out_specs = (
        P("ctx", None),
        P("ctx", None),
        P("exp", None, "ctx"),
        P("exp", "ctx", None),
        P("exp", None, None),
        P(),
        P(),
        P(),
    )
    return jax.shard_map(
        per_device, mesh=mesh, in_specs=in_specs, out_specs=out_specs, check_vma=False
    )
```

```python
import functools

import jax
import jax.numpy as jnp
from jax import lax
from jax.experimental import pallas as pl
from jax.experimental.pallas import tpu as pltpu
from jax.sharding import PartitionSpec as P

MOST = 8
GROUP = 2 * MOST
PARTS = 4
SIDE = 8
LANES = 128
GELU_C = 0.7978845608028654
MIB = 1 << 20
CHUNK = 256
SHARE = MIB // 2
EARLY = (1, 1, 2)
f32, bf16 = jnp.float32, jnp.bfloat16
WHOLE = pl.BlockSpec(memory_space=pltpu.VMEM)
SCALARS = pl.BlockSpec(memory_space=pltpu.SMEM)
ORDER = pl.BlockSpec(memory_space=pl.ANY)


def in_hbm(*arrays):
    return [pltpu.with_memory_space_constraint(array, pltpu.HBM) for array in arrays]


def fold_vector(row):
    return jnp.concatenate([row[:, k : k + LANES] for k in range(0, row.shape[1], LANES)], axis=0)


def spread(vector, rows):
    depth = vector.shape[0]
    if rows > depth:
        return jnp.concatenate([vector, jnp.zeros((rows - depth, LANES), f32)], axis=0)
    return jnp.concatenate([vector[k : k + rows] for k in range(0, depth, rows)], axis=1)


def spread_columns(width, rows):
    return LANES * max(1, width // LANES // rows)


def unspread(columns, width):
    rows = columns.shape[0]
    depth, each = width // LANES, spread_columns(width, rows)
    vectors = []
    for at in range(0, columns.shape[1], each):
        cuts = [columns[:, k : k + LANES] for k in range(at, at + each, LANES)]
        vectors.append(jnp.concatenate(cuts, axis=0)[:depth])
    return vectors


def start_copies(pairs, sems):
    copies = [pltpu.make_async_copy(a, b, sems.at[k]) for k, (a, b) in enumerate(pairs)]
    for copy in copies:
        copy.start()
    return copies


def dot(left, right, left_dim, right_dim):
    return lax.dot_general(
        left, right, (((left_dim,), (right_dim,)), ((), ())), preferred_element_type=f32
    )


def iota(shape, dim):
    return lax.broadcasted_iota(jnp.int32, shape, dim)


def select_body(place, picked_h, tokens_h, grads_h, own_o, other_o, ids_o, picked, tokens, grads, sems):
    tok_count = tokens.shape[0]
    pairs = [(picked_h, picked)]
    for k in range(PARTS):
        cut = pl.ds(k * (tok_count // PARTS), tok_count // PARTS)
        pairs += [(tokens_h.at[cut], tokens.at[cut]), (grads_h.at[cut], grads.at[cut])]
    copies = start_copies(pairs, sems)
    cap = picked.shape[2]
    start = place[0] * tok_count
    group = place[1]
    copies[0].wait()
    ids = picked[0].astype(f32)
    lanes, rows = iota((cap, cap), 1), iota((cap, cap), 0)
    eye = (lanes == rows).astype(f32)
    before = (rows < lanes).astype(f32)
    slot = (iota((GROUP, cap), 0) % MOST).astype(f32)
    tables = []
    for which in range(2):
        row = jnp.where(group == which, ids[0:1], ids[1:2]) - start.astype(f32)
        inside = ((row >= 0.0) & (row < float(tok_count))).astype(f32)
        inside_col = jnp.sum(eye * inside, axis=1, keepdims=True)
        local_col = jnp.sum(eye * row, axis=1, keepdims=True)
        rank = jnp.sum(before * inside_col, axis=0, keepdims=True)
        hit = jnp.where(rank == slot, 1.0, 0.0) * inside
        token_hit = (local_col == iota((cap, tok_count), 1).astype(f32)).astype(f32)
        tables.append(dot(hit, token_hit, 1, 0))
    table = jnp.concatenate(tables, axis=0).astype(bf16)
    second = (iota((2 * GROUP, 1), 0) % GROUP) >= MOST
    for copy in copies[1:]:
        copy.wait()
    rows = jnp.where(second, dot(table, grads[...], 1, 0), dot(table, tokens[...], 1, 0)).astype(bf16)
    own_o[...] = rows[:GROUP]
    other_o[...] = rows[GROUP:]
    number = (iota((SIDE, tok_count), 1) + 1).astype(bf16)
    ids_row = dot(number, table, 1, 1) - 1.0
    kind = (iota((SIDE, 2 * GROUP), 1) % GROUP) >= MOST
    want = iota((SIDE, 2 * GROUP), 0) == 1
    ids_o[...] = jnp.where(kind == want, ids_row, -1.0)


def select(place, picked, tokens, grads):
    width = tokens.shape[1]
    return pl.pallas_call(
        select_body,
        in_specs=[SCALARS] + [ORDER] * 3,
        out_specs=[WHOLE, WHOLE, WHOLE],
        scratch_shapes=[
            pltpu.VMEM(picked.shape, jnp.int32),
            pltpu.VMEM(tokens.shape, bf16),
            pltpu.VMEM(grads.shape, bf16),
            pltpu.SemaphoreType.DMA((1 + 2 * PARTS,)),
        ],
        out_shape=[
            jax.ShapeDtypeStruct((GROUP, width), bf16),
            jax.ShapeDtypeStruct((GROUP, width), bf16),
            jax.ShapeDtypeStruct((SIDE, 2 * GROUP), f32),
        ],
        compiler_params=pltpu.CompilerParams(vmem_limit_bytes=16 * MIB),
        name="select",
    )(place, *in_hbm(picked, tokens, grads))


def fetch(up_h, down_h, up, down, sems, first, count):
    pairs = []
    for k in range(count):
        here = pl.ds((first + k) * CHUNK, CHUNK)
        pairs += [(up_h.at[0, :, here], up.at[k]), (down_h.at[0, here, :], down.at[k])]
    return start_copies(pairs, sems)


def bring_body(first, up_h, down_h, _, up_o, down_o, done, sems):
    copies = fetch(up_h, down_h, up_o, down_o, sems, first, up_o.shape[0])
    done[...] = jnp.zeros_like(done)
    for copy in copies:
        copy.wait()


def bring(up, down, behind, first, count):
    width = up.shape[1]
    return pl.pallas_call(
        functools.partial(bring_body, first),
        in_specs=[ORDER] * 3,
        out_specs=[WHOLE] * 3,
        out_shape=[
            pltpu.VMEM((count, width, CHUNK), bf16),
            pltpu.VMEM((count, CHUNK, width), bf16),
            jax.ShapeDtypeStruct((8, 128), f32),
        ],
        scratch_shapes=[pltpu.SemaphoreType.DMA((2 * count,))],
        compiler_params=pltpu.CompilerParams(vmem_limit_bytes=8 * MIB),
        cost_estimate=pl.CostEstimate(flops=0, bytes_accessed=4 * count * width * CHUNK, transcendentals=0),
        name="bring",
    )(*in_hbm(up, down), behind)


def join_body(first, near_t, near_g, far_t, far_g, _, tokens_o, grads_o):
    if first:
        rows = [ref[...].astype(f32) for ref in (near_t, far_t)]
        tokens_o[...] = jnp.concatenate([r[:MOST] for r in rows], axis=0).astype(bf16)
        grads_o[...] = jnp.concatenate([r[MOST:] for r in rows], axis=0).astype(bf16)
    else:
        tokens_o[...] = jnp.concatenate([near_t[...], far_t[...]], axis=0)
        grads_o[...] = jnp.concatenate([near_g[...], far_g[...]], axis=0)


def join(first, near, far, behind):
    rows, width = near[0].shape
    rows = rows if first else 2 * rows
    return pl.pallas_call(
        functools.partial(join_body, first),
        in_specs=[WHOLE] * 4 + [ORDER],
        out_specs=[WHOLE] * 2,
        out_shape=[jax.ShapeDtypeStruct((rows, width), bf16)] * 2,
        compiler_params=pltpu.CompilerParams(vmem_limit_bytes=8 * MIB),
        name="join",
    )(*near, *far, behind)


def expert_body(
    places, counts, near_t, far_t, near_g, far_g, column, shift, one, gate, up_h, down_h, *refs
):
    early, refs = refs[:-16], refs[-16:]
    hid_o, grows_o, act_o, gpre_o, eo_keep, back_keep, eo_send, back_send, side_o = refs[:9]
    normed_s, eo_s, back_s, weight_s, up_s, down_s, sems = refs[9:]
    width = hid_o.shape[1]
    blocks = len(places)
    half = blocks // 2
    chunk = up_s.shape[2]
    at_hand = [(up.at[k], down.at[k]) for up, down in zip(early[::2], early[1::2]) for k in range(up.shape[0])]
    steps = up_h.shape[2] // chunk
    late = fetch(up_h, down_h, up_s, down_s, sems, len(at_hand), steps - len(at_hand))

    def pair(near, far, block):
        at = MOST * (block % half)
        return (near if block < half else far).at[at : at + GROUP, :]

    place = iota((GROUP, 1), 0)
    for block in range(0, blocks, 2):
        tok = pair(near_t, far_t, block)[...].astype(f32)
        grd = pair(near_g, far_g, places[block])[...].astype(f32)
        rows = pl.ds(block * MOST, GROUP)
        limit = jnp.where(place < MOST, counts[block], counts[block + 1] + MOST)
        filled = (place < limit).astype(f32)
        centered = tok - jnp.mean(tok, axis=1, keepdims=True)
        inverse_std = lax.rsqrt(jnp.mean(centered * centered, axis=1, keepdims=True) + 1e-06)
        normed = centered * inverse_std
        normed_s[rows, :] = normed
        hidden = ((normed * one[...] + shift[...]) * filled).astype(bf16)
        hid_o[rows, :] = hidden
        logit = jnp.sum(hidden.astype(f32) * column[...], axis=1, keepdims=True)
        weight = 1.0 / (1.0 + jnp.exp(-logit))
        weight_s[rows, :] = jnp.broadcast_to(weight, (GROUP, 128))
        grows_o[rows, :] = (weight * (gate[...] * grd)).astype(bf16)

    for step in range(steps):
        here = pl.ds(step * chunk, chunk)
        if step < len(at_hand):
            up_block, down_block = [ref[...] for ref in at_hand[step]]
        else:
            k = step - len(at_hand)
            late[2 * k].wait()
            late[2 * k + 1].wait()
            up_block, down_block = up_s[k], down_s[k]
        pre = dot(hid_o[...], up_block, 1, 0)
        grad_act = dot(grows_o[...], down_block, 1, 1)
        square = pre * pre
        tangent = jnp.tanh(GELU_C * (pre + 0.044715 * square * pre))
        act = (0.5 * pre * (1.0 + tangent)).astype(bf16)
        slope = 0.5 * (1.0 + tangent) + 0.5 * pre * (1.0 - tangent * tangent) * GELU_C * (
            1.0 + 3.0 * 0.044715 * square
        )
        grad_pre = (grad_act * slope).astype(bf16)
        act_o[:, here] = act
        gpre_o[:, here] = grad_pre
        eo, back = dot(act, down_block, 1, 0), dot(grad_pre, up_block, 1, 1)
        if step == 0:
            eo_s[...] = eo
            back_s[...] = back
        else:
            eo_s[...] += eo
            back_s[...] += back

    gate_v = shift_v = scale_v = router_v = jnp.zeros((1, width), f32)
    for block in range(0, blocks, 2):
        grd = pair(near_g, far_g, places[block])[...].astype(f32)
        rows = pl.ds(block * MOST, GROUP)
        weight = weight_s[rows, 0:1]
        eo = eo_s[rows, :]
        grad_logit = jnp.sum(gate[...] * grd * eo, axis=1, keepdims=True) * weight * (1.0 - weight)
        eo = weight * eo
        back = back_s[rows, :] + grad_logit * column[...]
        gate_v += jnp.sum(grd * eo, axis=0, keepdims=True)
        shift_v += jnp.sum(back, axis=0, keepdims=True)
        scale_v += jnp.sum(back * normed_s[rows, :], axis=0, keepdims=True)
        router_v += jnp.sum(grad_logit * hid_o[rows, :].astype(f32), axis=0, keepdims=True)
        for values, keep, send, at in ((eo, eo_keep, eo_send, block), (back, back_keep, back_send, places[block])):
            if at < half:
                pair(keep, None, at)[...] = values
            else:
                here = MOST * (at % half)
                send[here : here + GROUP, :width] = values.astype(bf16)
    sums = [fold_vector(row) for row in (gate_v, shift_v, scale_v, router_v)]
    side_o[...] = jnp.concatenate(sums, axis=0)
    rows = eo_send.shape[0]
    eo_send[:, width:] = jnp.concatenate([spread(v, rows) for v in sums[:2]], axis=1).astype(bf16)
    back_send[:, width:] = jnp.concatenate([spread(v, rows) for v in sums[2:]], axis=1).astype(bf16)


def experts(places, counts, near_t, far_t, near_g, far_g, shift, one, gate, column, up, down, early):
    blocks = counts.shape[0]
    slot_count = blocks * MOST
    width, hid_count = up.shape[1], up.shape[2]
    late = max(1, hid_count // CHUNK - sum(part.shape[0] for part in early[::2]))
    rows = MOST * blocks // 2
    return pl.pallas_call(
        functools.partial(expert_body, places),
        in_specs=[SCALARS] + [WHOLE] * 8 + [ORDER] * 2 + [WHOLE] * len(early),
        out_specs=[WHOLE] * 9,
        out_shape=[
            jax.ShapeDtypeStruct((slot_count, width), bf16),
            jax.ShapeDtypeStruct((slot_count, width), bf16),
            jax.ShapeDtypeStruct((slot_count, hid_count), bf16),
            jax.ShapeDtypeStruct((slot_count, hid_count), bf16),
            jax.ShapeDtypeStruct((rows, width), f32),
            jax.ShapeDtypeStruct((rows, width), f32),
            jax.ShapeDtypeStruct((rows, width + 2 * spread_columns(width, rows)), bf16),
            jax.ShapeDtypeStruct((rows, width + 2 * spread_columns(width, rows)), bf16),
            jax.ShapeDtypeStruct((4 * width // LANES, LANES), f32),
        ],
        scratch_shapes=[pltpu.VMEM((slot_count, width), f32)] * 3
        + [pltpu.VMEM((slot_count, 128), f32)]
        + [pltpu.VMEM((late, width, CHUNK), bf16), pltpu.VMEM((late, CHUNK, width), bf16)]
        + [pltpu.SemaphoreType.DMA((2 * late,))],
        compiler_params=pltpu.CompilerParams(vmem_limit_bytes=(12 * max(1, slot_count // 64) + 4 * late) * MIB),
        cost_estimate=pl.CostEstimate(
            flops=8 * slot_count * width * hid_count, bytes_accessed=4 * width * hid_count, transcendentals=0
        ),
        name="experts",
    )(counts, near_t, far_t, near_g, far_g, column, shift, one, gate, *in_hbm(up, down), *early)


def outer_body(step, left, right, *refs):
    out_h, done, out, sems = refs[-4:]
    done[...] = jnp.zeros_like(done)
    first = refs[-5]
    copies = []
    for k in range(out.shape[0] // step):
        here = pl.ds(k * step, step)
        out[here, :] = dot(left[:, first + k * step : first + (k + 1) * step], right[...], 0, 0).astype(bf16)
        copies += start_copies([(out.at[here], out_h.at[0, pl.ds(first + k * step, step)])], sems.at[pl.ds(k, 1)])
    for copy in copies:
        copy.wait()


def outer(left, right, behind, name, first, count, into=None):
    depth, rows = left.shape
    columns = right.shape[1]
    share = count * rows // 4
    step = min(rows // 4, SHARE // columns)
    before = [] if into is None else [into]

    def body(left, right, _, *refs):
        outer_body(step, left, right, first * rows // 4, *refs[-4:])

    return pl.pallas_call(
        body,
        in_specs=[WHOLE] * 2 + [ORDER] * (1 + len(before)),
        out_specs=[ORDER, WHOLE],
        out_shape=[jax.ShapeDtypeStruct((1, rows, columns), bf16), jax.ShapeDtypeStruct((8, 128), f32)],
        scratch_shapes=[pltpu.VMEM((share, columns), bf16), pltpu.SemaphoreType.DMA((share // step,))],
        input_output_aliases={3: 0} if before else {},
        compiler_params=pltpu.CompilerParams(vmem_limit_bytes=24 * MIB),
        cost_estimate=pl.CostEstimate(
            flops=2 * depth * rows * columns * count, bytes_accessed=rows * columns * count, transcendentals=0
        ),
        name=name,
    )(left, right, behind, *before)


def number_columns(ids, rows):
    blank = jnp.full((SIDE, LANES - ids.shape[1]), -1.0, f32)
    numbers = jnp.concatenate([ids, blank], axis=1)
    return jnp.concatenate([numbers, jnp.zeros((rows - SIDE, LANES), f32)], axis=0)


def fold_body(last, keep_e, keep_b, got_e, got_b, side, ids, _, *outs):
    rows, width = keep_e.shape
    depth = width // LANES
    got = [got_e[...].astype(f32), got_b[...].astype(f32)]
    eo = keep_e[...] + got[0][:, :width]
    back = keep_b[...] + got[1][:, :width]
    theirs = unspread(got[0][:, width:], width) + unspread(got[1][:, width:], width)
    sums = [side[k * depth : (k + 1) * depth] + v for k, v in enumerate(theirs)]
    outs[0][...] = jnp.concatenate(sums, axis=0)
    low, high = slice(0, rows // 2), slice(rows // 2, rows)
    if last:
        mine = jnp.concatenate([eo[low], back[low]], axis=0)
        outs[1][...] = jnp.concatenate([mine, number_columns(ids[:, :rows], rows)], axis=1).astype(bf16)
        send = jnp.concatenate([eo[high], back[high]], axis=0)
        outs[2][...] = jnp.concatenate([send] + [spread(v, rows) for v in sums], axis=1).astype(bf16)
    else:
        outs[1][...] = eo[low]
        outs[2][...] = back[low]
        outs[3][...] = jnp.concatenate([eo[high]] + [spread(v, rows // 2) for v in sums[:2]], axis=1).astype(bf16)
        outs[4][...] = jnp.concatenate([back[high]] + [spread(v, rows // 2) for v in sums[2:]], axis=1).astype(bf16)


def fold(keep, got, side, ids, behind):
    rows, width = keep[0].shape
    last = rows == 2 * MOST
    shapes = [(side.shape, f32)]
    if last:
        shapes += [((rows, width + LANES), bf16), ((rows, width + 4 * spread_columns(width, rows)), bf16)]
    else:
        wide = width + 2 * spread_columns(width, rows // 2)
        shapes += [((rows // 2, width), f32)] * 2 + [((rows // 2, wide), bf16)] * 2
    return pl.pallas_call(
        functools.partial(fold_body, last),
        in_specs=[WHOLE] * 6 + [ORDER],
        out_specs=[WHOLE] * len(shapes),
        out_shape=[jax.ShapeDtypeStruct(shape, kind) for shape, kind in shapes],
        compiler_params=pltpu.CompilerParams(vmem_limit_bytes=16 * MIB),
        name="fold",
    )(*keep, *got, side, ids, behind)


def pack_body(width, got, side, ids, *refs):
    mine_o = refs[-1]
    depth = width // LANES
    theirs = got[...].astype(f32)
    sums = [side[k * depth : (k + 1) * depth] + v for k, v in enumerate(unspread(theirs[:, width:], width)[:3])]
    rows = mine_o.shape[0]
    numbers = number_columns(ids[:, rows:], rows)
    mine_o[...] = jnp.concatenate(
        [theirs[:, :width]] + [spread(v, rows) for v in sums] + [numbers], axis=1
    ).astype(bf16)


def pack(width, got, side, ids, *behind):
    rows = got.shape[0]
    return pl.pallas_call(
        functools.partial(pack_body, width),
        in_specs=[WHOLE] * 3 + [ORDER] * len(behind),
        out_specs=WHOLE,
        out_shape=jax.ShapeDtypeStruct((rows, width + 3 * spread_columns(width, rows) + LANES), bf16),
        compiler_params=pltpu.CompilerParams(vmem_limit_bytes=16 * MIB),
        name="pack",
    )(got, side, ids, *behind)


def relay_body(rows, *refs):
    refs[-1][...] = rows[...]


def relay(rows, *behind):
    return pl.pallas_call(
        relay_body,
        in_specs=[WHOLE] + [ORDER] * len(behind),
        out_specs=WHOLE,
        out_shape=jax.ShapeDtypeStruct(rows.shape, rows.dtype),
        compiler_params=pltpu.CompilerParams(vmem_limit_bytes=16 * MIB),
        name="relay",
    )(rows, *behind)


def normalize_body(tokens, grads, shift, scale, gate, normed_o, inverse_o, tokens_o, grads_o, shift_o, one_o, gate_o):
    inputs = tokens[...].astype(f32)
    centered = inputs - jnp.mean(inputs, axis=1, keepdims=True)
    inverse_std = lax.rsqrt(jnp.mean(centered * centered, axis=1, keepdims=True) + 1e-06)
    normed_o[...] = centered * inverse_std
    inverse_o[...] = jnp.broadcast_to(inverse_std, inverse_o.shape)
    tokens_o[...] = tokens[...]
    grads_o[...] = grads[...]
    shift_o[...] = shift[...]
    one_o[...] = 1.0 + scale[...]
    gate_o[...] = gate[...]


def normalize(tokens, grads, shift, scale, gate):
    tok_count, width = tokens.shape
    step = min(tok_count, 32)
    wide = pl.BlockSpec((step, width), lambda i: (i, 0))
    narrow = pl.BlockSpec((step, 128), lambda i: (i, 0))
    line = pl.BlockSpec((1, width), lambda i: (0, 0))
    return pl.pallas_call(
        normalize_body,
        grid=(tok_count // step,),
        in_specs=[wide, wide, line, line, line],
        out_specs=[wide, narrow, wide, wide, line, line, line],
        out_shape=[
            jax.ShapeDtypeStruct((tok_count, width), f32),
            jax.ShapeDtypeStruct((tok_count, 128), f32),
            jax.ShapeDtypeStruct((tok_count, width), bf16),
            jax.ShapeDtypeStruct((tok_count, width), bf16),
        ]
        + [jax.ShapeDtypeStruct((1, width), f32)] * 3,
        compiler_params=pltpu.CompilerParams(vmem_limit_bytes=16 * MIB),
        cost_estimate=pl.CostEstimate(flops=10 * tok_count * width, bytes_accessed=6 * tok_count * width, transcendentals=0),
        name="normalize",
    )(*in_hbm(tokens, grads, shift, scale, gate))


def finish_body(
    parts, place, side, got, inverse, tokens, grads, normed, one, gate, *refs
):
    pieces = refs[:-14]
    block_h, tgrad_h, gate_h, shift_h, scale_h, router_h = refs[-14:-8]
    gate_s, shift_s, scale_s, router_s, block_s, tgrad_s, vector_sems, out_sems = refs[-8:]
    total = tokens.shape[0]
    count = total // parts
    cuts = [pl.ds(k * count, count) for k in range(parts)]
    width = tokens.shape[1]
    depth = width // LANES
    rows = jnp.concatenate([piece[:, :width] for piece in pieces], axis=0)
    ids = [piece[:, piece.shape[1] - LANES :].astype(f32)[:, : piece.shape[0]] for piece in pieces]
    ids = [jnp.concatenate([each[kind : 1 + kind] for each in ids], axis=1) for kind in range(2)]
    with_sums = [piece for piece in pieces if piece.shape[1] > width + LANES]
    vector = sum(piece[:, width : piece.shape[1] - LANES].astype(f32) for piece in with_sums)
    gate_s[...], shift_s[...], scale_s[...] = unspread(vector, width)
    own = side[3 * depth :]
    other = unspread(got[...].astype(f32)[:, width:], width)[3]
    first = place[1] == 0
    for k, row in enumerate((jnp.where(first, own, other), jnp.where(first, other, own))):
        router_s[k : k + 1] = jnp.concatenate([row[at : at + 1] for at in range(depth)], axis=1)
    departures = start_copies(
        ((gate_s, gate_h), (shift_s, shift_h), (scale_s, scale_h), (router_s, router_h)), vector_sems
    )
    for k, cut in enumerate(cuts):
        numbers = (iota((count, rows.shape[0]), 0) + k * count).astype(f32)
        table = jnp.concatenate([(numbers == each).astype(f32) for each in ids], axis=0)
        sums = dot(table.astype(bf16), rows, 1, 0)
        block_s[cut, :] = (tokens[cut, :].astype(f32) + gate[...] * sums[:count]).astype(bf16)
        grad_norm = sums[count:] * one[...]
        center = jnp.mean(grad_norm, axis=1, keepdims=True)
        along = jnp.mean(grad_norm * normed[cut, :], axis=1, keepdims=True)
        tgrad_s[cut, :] = (
            grads[cut, :].astype(f32) + inverse[cut, 0:1] * (grad_norm - center - normed[cut, :] * along)
        ).astype(bf16)
        departures += start_copies(((block_s.at[cut], block_h.at[cut]), (tgrad_s.at[cut], tgrad_h.at[cut])), out_sems.at[k])
    for copy in departures:
        copy.wait()


def finish(place, side, got, pieces, one, gate, tokens, grads, normed, inverse):
    tok_count, width = tokens.shape
    parts = 4
    vector = jax.ShapeDtypeStruct((width // LANES, LANES), f32)
    return pl.pallas_call(
        functools.partial(finish_body, parts),
        in_specs=[SCALARS] + [WHOLE] * (8 + len(pieces)),
        out_specs=[ORDER] * 6,
        out_shape=[jax.ShapeDtypeStruct((tok_count, width), bf16)] * 2
        + [vector] * 3
        + [jax.ShapeDtypeStruct((2, width), f32)],
        scratch_shapes=[pltpu.VMEM(vector.shape, f32)] * 3
        + [pltpu.VMEM((2, width), f32)]
        + [pltpu.VMEM((tok_count, width), kind) for kind in (bf16, bf16)]
        + [pltpu.SemaphoreType.DMA(shape) for shape in ((4,), (parts, 2))],
        compiler_params=pltpu.CompilerParams(vmem_limit_bytes=24 * MIB),
        name="finish",
    )(place, side, got, inverse, tokens, grads, normed, one, gate, *pieces)


def swap(values, axis, mask):
    size = lax.axis_size(axis)
    return lax.ppermute(values, axis, [(i, i ^ mask) for i in range(size)])


def halvings(size):
    masks = []
    while size > 1:
        size //= 2
        masks.append(size)
    return masks


def per_device(
    tokens, ada_shift, ada_scale, ada_gate, router, expert_up, expert_down, picked_ids, out_grad
):
    tok_count, width = tokens.shape
    ctx_size, exp_size = lax.axis_size("ctx"), lax.axis_size("exp")
    ctx_masks, exp_masks = halvings(ctx_size), halvings(exp_size)
    me = lax.axis_index("ctx")
    group = me // ctx_masks[0]
    picked = picked_ids[0]
    shift, scale, gate = ada_shift[None], ada_scale[None], ada_gate[None]
    place = jnp.stack([me, group]).astype(jnp.int32)
    own, other, ids = select(place, picked_ids, tokens, out_grad)

    orders = ctx_masks[1:], ctx_masks[:0:-1]
    relative = []
    for order in orders:
        blocks = [0]
        for mask in [ctx_masks[0], *order]:
            blocks = blocks + [r ^ mask for r in blocks]
        relative.append(blocks)
    places = [relative[1].index(r) for r in relative[0]]
    sources = me ^ jnp.array(relative[0], jnp.int32)
    own_ids = jnp.where(group == 0, picked[0], picked[1])
    counts = jnp.sum((own_ids // tok_count)[None, :] == sources[:, None], axis=1).astype(jnp.int32)
    columns = router[0].astype(f32).T
    column = jnp.where(group == 0, columns[0:1], columns[1:2])

    normed, inverse, near_tokens, near_grads, shift, one, gate = normalize(tokens, out_grad, shift, scale, gate)
    early, brought, behind = [], 0, own

    def bring_some(step):
        nonlocal brought, behind
        count = min(EARLY[step] if step < len(EARLY) else 0, expert_up.shape[2] // CHUNK - brought)
        if count > 0:
            *weights, behind = bring(expert_up, expert_down, behind, brought, count)
            early.extend(weights)
            brought += count

    got = swap(other, "ctx", ctx_masks[0])
    bring_some(0)
    near = join(True, [own, own], [got, got], behind)
    far = [swap(near[k], "ctx", orders[k][0]) for k in range(2)]
    for step, masks in enumerate(zip(orders[0][1:], orders[1][1:])):
        behind = near[0]
        bring_some(1 + step)
        near = join(False, near, far, behind)
        far = [swap(near[k], "ctx", masks[k]) for k in range(2)]
    behind = near[0]
    bring_some(len(orders[0]))
    hidden, grad_rows, act, grad_pre, eo_keep, back_keep, eo_send, back_send, side = experts(
        places, counts, near[0], far[0], near[1], far[1], shift, one, gate, column, expert_up, expert_down, early
    )

    rows = eo_keep.shape[0]
    keep, send = [eo_keep, back_keep], [eo_send, back_send]
    behind = side
    for step, masks in enumerate(zip(orders[0][::-1], orders[1][::-1])):
        got = [swap(send[k], "ctx", masks[k]) for k in range(2)]
        if step == 0:
            up_grad, behind = outer(hidden, grad_pre, behind, "up_grad", 0, 4)
        elif step == 1:
            down_grad, behind = outer(act, grad_rows, behind, "down_grad", 0, 2)
        side, *rest = fold(keep, got, side, ids, behind)
        keep, send = rest[:-2], rest[-2:]
        behind = side
    mine, send = rest
    got = swap(send, "ctx", ctx_masks[0])
    down_grad, behind = outer(act, grad_rows, behind, "down_grad", 2, 1, down_grad)
    come = swap(mine, "exp", exp_masks[0])
    pieces = [mine, come]
    mine = pack(width, got, side, ids, behind)
    come = swap(mine, "exp", exp_masks[0])
    down_grad, behind = outer(act, grad_rows, mine, "down_grad", 3, 1, down_grad)
    for mask in exp_masks[1:]:
        pieces = pieces + [swap(piece, "exp", mask) for piece in pieces]
    last = [mine, relay(come, behind, *pieces[2:])]
    for mask in exp_masks[1:]:
        last = last + [swap(piece, "exp", mask) for piece in last]
    pieces = pieces + last
    block_out, tokens_grad, gate_grad, shift_grad, scale_grad, router_rows = finish(
        place, side, got, pieces, one, gate, near_tokens, near_grads, normed, inverse
    )
    return (
        block_out,
        tokens_grad,
        up_grad,
        down_grad,
        router_rows.T[None],
        shift_grad.reshape(width),
        scale_grad.reshape(width),
        gate_grad.reshape(width),
    )


def solution(mesh):
    in_specs = (
        P("ctx", None),
        P(),
        P(),
        P(),
        P("exp", None, None),
        P("exp", None, "ctx"),
        P("exp", "ctx", None),
        P("exp", None, None),
        P("ctx", None),
    )
    out_specs = (
        P("ctx", None),
        P("ctx", None),
        P("exp", None, "ctx"),
        P("exp", "ctx", None),
        P("exp", None, None),
        P(),
        P(),
        P(),
    )
    return jax.shard_map(
        per_device, mesh=mesh, in_specs=in_specs, out_specs=out_specs, check_vma=False
    )
```

```python
import functools

import jax
import jax.numpy as jnp
from jax import lax
from jax.experimental import pallas as pl
from jax.experimental.pallas import tpu as pltpu
from jax.sharding import PartitionSpec as P

MOST = 8
GROUP = 2 * MOST
PARTS = 4
SIDE = 8
LANES = 128
GELU_C = 0.7978845608028654
MIB = 1 << 20
CHUNK = 256
SHARE = MIB // 2
EARLY = (1, 1, 2)
f32, bf16 = jnp.float32, jnp.bfloat16
WHOLE = pl.BlockSpec(memory_space=pltpu.VMEM)
SCALARS = pl.BlockSpec(memory_space=pltpu.SMEM)
ORDER = pl.BlockSpec(memory_space=pl.ANY)


def in_hbm(*arrays):
    return [pltpu.with_memory_space_constraint(array, pltpu.HBM) for array in arrays]


def fold_vector(row):
    return jnp.concatenate([row[:, k : k + LANES] for k in range(0, row.shape[1], LANES)], axis=0)


def spread(vector, rows):
    depth = vector.shape[0]
    if rows > depth:
        return jnp.concatenate([vector, jnp.zeros((rows - depth, LANES), f32)], axis=0)
    return jnp.concatenate([vector[k : k + rows] for k in range(0, depth, rows)], axis=1)


def spread_columns(width, rows):
    return LANES * max(1, width // LANES // rows)


def unspread(columns, width):
    rows = columns.shape[0]
    depth, each = width // LANES, spread_columns(width, rows)
    vectors = []
    for at in range(0, columns.shape[1], each):
        cuts = [columns[:, k : k + LANES] for k in range(at, at + each, LANES)]
        vectors.append(jnp.concatenate(cuts, axis=0)[:depth])
    return vectors


def start_copies(pairs, sems):
    copies = [pltpu.make_async_copy(a, b, sems.at[k]) for k, (a, b) in enumerate(pairs)]
    for copy in copies:
        copy.start()
    return copies


def dot(left, right, left_dim, right_dim):
    return lax.dot_general(
        left, right, (((left_dim,), (right_dim,)), ((), ())), preferred_element_type=f32
    )


def iota(shape, dim):
    return lax.broadcasted_iota(jnp.int32, shape, dim)


def select_body(place, picked_h, tokens_h, grads_h, own_o, other_o, ids_o, picked, tokens, grads, sems):
    tok_count = tokens.shape[0]
    pairs = [(picked_h, picked)]
    for k in range(PARTS):
        cut = pl.ds(k * (tok_count // PARTS), tok_count // PARTS)
        pairs += [(tokens_h.at[cut], tokens.at[cut]), (grads_h.at[cut], grads.at[cut])]
    copies = start_copies(pairs, sems)
    cap = picked.shape[2]
    start = place[0] * tok_count
    group = place[1]
    copies[0].wait()
    ids = picked[0].astype(f32)
    lanes, rows = iota((cap, cap), 1), iota((cap, cap), 0)
    eye = (lanes == rows).astype(f32)
    before = (rows < lanes).astype(f32)
    slot = (iota((GROUP, cap), 0) % MOST).astype(f32)
    tables = []
    for which in range(2):
        row = jnp.where(group == which, ids[0:1], ids[1:2]) - start.astype(f32)
        inside = ((row >= 0.0) & (row < float(tok_count))).astype(f32)
        inside_col = jnp.sum(eye * inside, axis=1, keepdims=True)
        local_col = jnp.sum(eye * row, axis=1, keepdims=True)
        rank = jnp.sum(before * inside_col, axis=0, keepdims=True)
        hit = jnp.where(rank == slot, 1.0, 0.0) * inside
        token_hit = (local_col == iota((cap, tok_count), 1).astype(f32)).astype(f32)
        tables.append(dot(hit, token_hit, 1, 0))
    table = jnp.concatenate(tables, axis=0).astype(bf16)
    second = (iota((2 * GROUP, 1), 0) % GROUP) >= MOST
    for copy in copies[1:]:
        copy.wait()
    rows = jnp.where(second, dot(table, grads[...], 1, 0), dot(table, tokens[...], 1, 0)).astype(bf16)
    own_o[...] = rows[:GROUP]
    other_o[...] = rows[GROUP:]
    number = (iota((SIDE, tok_count), 1) + 1).astype(bf16)
    ids_row = dot(number, table, 1, 1) - 1.0
    kind = (iota((SIDE, 2 * GROUP), 1) % GROUP) >= MOST
    want = iota((SIDE, 2 * GROUP), 0) == 1
    ids_o[...] = jnp.where(kind == want, ids_row, -1.0)


def select(place, picked, tokens, grads):
    width = tokens.shape[1]
    return pl.pallas_call(
        select_body,
        in_specs=[SCALARS] + [ORDER] * 3,
        out_specs=[WHOLE, WHOLE, WHOLE],
        scratch_shapes=[
            pltpu.VMEM(picked.shape, jnp.int32),
            pltpu.VMEM(tokens.shape, bf16),
            pltpu.VMEM(grads.shape, bf16),
            pltpu.SemaphoreType.DMA((1 + 2 * PARTS,)),
        ],
        out_shape=[
            jax.ShapeDtypeStruct((GROUP, width), bf16),
            jax.ShapeDtypeStruct((GROUP, width), bf16),
            jax.ShapeDtypeStruct((SIDE, 2 * GROUP), f32),
        ],
        compiler_params=pltpu.CompilerParams(vmem_limit_bytes=16 * MIB),
        name="select",
    )(place, *in_hbm(picked, tokens, grads))


def fetch(up_h, down_h, up, down, sems, first, count):
    pairs = []
    for k in range(count):
        here = pl.ds((first + k) * CHUNK, CHUNK)
        pairs += [(up_h.at[0, :, here], up.at[k]), (down_h.at[0, here, :], down.at[k])]
    return start_copies(pairs, sems)


def bring_body(first, up_h, down_h, _, up_o, down_o, done, sems):
    copies = fetch(up_h, down_h, up_o, down_o, sems, first, up_o.shape[0])
    done[...] = jnp.zeros_like(done)
    for copy in copies:
        copy.wait()


def bring(up, down, behind, first, count):
    width = up.shape[1]
    return pl.pallas_call(
        functools.partial(bring_body, first),
        in_specs=[ORDER] * 3,
        out_specs=[WHOLE] * 3,
        out_shape=[
            pltpu.VMEM((count, width, CHUNK), bf16),
            pltpu.VMEM((count, CHUNK, width), bf16),
            jax.ShapeDtypeStruct((8, 128), f32),
        ],
        scratch_shapes=[pltpu.SemaphoreType.DMA((2 * count,))],
        compiler_params=pltpu.CompilerParams(vmem_limit_bytes=8 * MIB),
        cost_estimate=pl.CostEstimate(flops=0, bytes_accessed=4 * count * width * CHUNK, transcendentals=0),
        name="bring",
    )(*in_hbm(up, down), behind)


def join_body(first, near_t, near_g, far_t, far_g, _, tokens_o, grads_o):
    if first:
        rows = [ref[...].astype(f32) for ref in (near_t, far_t)]
        tokens_o[...] = jnp.concatenate([r[:MOST] for r in rows], axis=0).astype(bf16)
        grads_o[...] = jnp.concatenate([r[MOST:] for r in rows], axis=0).astype(bf16)
    else:
        tokens_o[...] = jnp.concatenate([near_t[...], far_t[...]], axis=0)
        grads_o[...] = jnp.concatenate([near_g[...], far_g[...]], axis=0)


def join(first, near, far, behind):
    rows, width = near[0].shape
    rows = rows if first else 2 * rows
    return pl.pallas_call(
        functools.partial(join_body, first),
        in_specs=[WHOLE] * 4 + [ORDER],
        out_specs=[WHOLE] * 2,
        out_shape=[jax.ShapeDtypeStruct((rows, width), bf16)] * 2,
        compiler_params=pltpu.CompilerParams(vmem_limit_bytes=8 * MIB),
        name="join",
    )(*near, *far, behind)


def expert_body(
    places, counts, near_t, far_t, near_g, far_g, column, shift, one, gate, up_h, down_h, *refs
):
    early, refs = refs[:-16], refs[-16:]
    hid_o, grows_o, act_o, gpre_o, eo_keep, back_keep, eo_send, back_send, side_o = refs[:9]
    normed_s, eo_s, back_s, weight_s, up_s, down_s, sems = refs[9:]
    width = hid_o.shape[1]
    blocks = len(places)
    half = blocks // 2
    chunk = up_s.shape[2]
    at_hand = [(up.at[k], down.at[k]) for up, down in zip(early[::2], early[1::2]) for k in range(up.shape[0])]
    steps = up_h.shape[2] // chunk
    late = fetch(up_h, down_h, up_s, down_s, sems, len(at_hand), steps - len(at_hand))

    def pair(near, far, block):
        at = MOST * (block % half)
        return (near if block < half else far).at[at : at + GROUP, :]

    place = iota((GROUP, 1), 0)
    for block in range(0, blocks, 2):
        tok = pair(near_t, far_t, block)[...].astype(f32)
        grd = pair(near_g, far_g, places[block])[...].astype(f32)
        rows = pl.ds(block * MOST, GROUP)
        limit = jnp.where(place < MOST, counts[block], counts[block + 1] + MOST)
        filled = (place < limit).astype(f32)
        centered = tok - jnp.mean(tok, axis=1, keepdims=True)
        inverse_std = lax.rsqrt(jnp.mean(centered * centered, axis=1, keepdims=True) + 1e-06)
        normed = centered * inverse_std
        normed_s[rows, :] = normed
        hidden = ((normed * one[...] + shift[...]) * filled).astype(bf16)
        hid_o[rows, :] = hidden
        logit = jnp.sum(hidden.astype(f32) * column[...], axis=1, keepdims=True)
        weight = 1.0 / (1.0 + jnp.exp(-logit))
        weight_s[rows, :] = jnp.broadcast_to(weight, (GROUP, 128))
        grows_o[rows, :] = (weight * (gate[...] * grd)).astype(bf16)

    for step in range(steps):
        here = pl.ds(step * chunk, chunk)
        if step < len(at_hand):
            up_block, down_block = [ref[...] for ref in at_hand[step]]
        else:
            k = step - len(at_hand)
            late[2 * k].wait()
            late[2 * k + 1].wait()
            up_block, down_block = up_s[k], down_s[k]
        pre = dot(hid_o[...], up_block, 1, 0)
        grad_act = dot(grows_o[...], down_block, 1, 1)
        square = pre * pre
        tangent = jnp.tanh(GELU_C * (pre + 0.044715 * square * pre))
        act = (0.5 * pre * (1.0 + tangent)).astype(bf16)
        slope = 0.5 * (1.0 + tangent) + 0.5 * pre * (1.0 - tangent * tangent) * GELU_C * (
            1.0 + 3.0 * 0.044715 * square
        )
        grad_pre = (grad_act * slope).astype(bf16)
        act_o[:, here] = act
        gpre_o[:, here] = grad_pre
        eo, back = dot(act, down_block, 1, 0), dot(grad_pre, up_block, 1, 1)
        if step == 0:
            eo_s[...] = eo
            back_s[...] = back
        else:
            eo_s[...] += eo
            back_s[...] += back

    gate_v = shift_v = scale_v = router_v = jnp.zeros((1, width), f32)
    for block in range(0, blocks, 2):
        grd = pair(near_g, far_g, places[block])[...].astype(f32)
        rows = pl.ds(block * MOST, GROUP)
        weight = weight_s[rows, 0:1]
        eo = eo_s[rows, :]
        grad_logit = jnp.sum(gate[...] * grd * eo, axis=1, keepdims=True) * weight * (1.0 - weight)
        eo = weight * eo
        back = back_s[rows, :] + grad_logit * column[...]
        gate_v += jnp.sum(grd * eo, axis=0, keepdims=True)
        shift_v += jnp.sum(back, axis=0, keepdims=True)
        scale_v += jnp.sum(back * normed_s[rows, :], axis=0, keepdims=True)
        router_v += jnp.sum(grad_logit * hid_o[rows, :].astype(f32), axis=0, keepdims=True)
        for values, keep, send, at in ((eo, eo_keep, eo_send, block), (back, back_keep, back_send, places[block])):
            if at < half:
                pair(keep, None, at)[...] = values
            else:
                here = MOST * (at % half)
                send[here : here + GROUP, :width] = values.astype(bf16)
    sums = [fold_vector(row) for row in (gate_v, shift_v, scale_v, router_v)]
    side_o[...] = jnp.concatenate(sums, axis=0)
    rows = eo_send.shape[0]
    eo_send[:, width:] = jnp.concatenate([spread(v, rows) for v in sums[:2]], axis=1).astype(bf16)
    back_send[:, width:] = jnp.concatenate([spread(v, rows) for v in sums[2:]], axis=1).astype(bf16)


def experts(places, counts, near_t, far_t, near_g, far_g, shift, one, gate, column, up, down, early):
    blocks = counts.shape[0]
    slot_count = blocks * MOST
    width, hid_count = up.shape[1], up.shape[2]
    late = max(1, hid_count // CHUNK - sum(part.shape[0] for part in early[::2]))
    rows = MOST * blocks // 2
    return pl.pallas_call(
        functools.partial(expert_body, places),
        in_specs=[SCALARS] + [WHOLE] * 8 + [ORDER] * 2 + [WHOLE] * len(early),
        out_specs=[WHOLE] * 9,
        out_shape=[
            jax.ShapeDtypeStruct((slot_count, width), bf16),
            jax.ShapeDtypeStruct((slot_count, width), bf16),
            jax.ShapeDtypeStruct((slot_count, hid_count), bf16),
            jax.ShapeDtypeStruct((slot_count, hid_count), bf16),
            jax.ShapeDtypeStruct((rows, width), f32),
            jax.ShapeDtypeStruct((rows, width), f32),
            jax.ShapeDtypeStruct((rows, width + 2 * spread_columns(width, rows)), bf16),
            jax.ShapeDtypeStruct((rows, width + 2 * spread_columns(width, rows)), bf16),
            jax.ShapeDtypeStruct((4 * width // LANES, LANES), f32),
        ],
        scratch_shapes=[pltpu.VMEM((slot_count, width), f32)] * 3
        + [pltpu.VMEM((slot_count, 128), f32)]
        + [pltpu.VMEM((late, width, CHUNK), bf16), pltpu.VMEM((late, CHUNK, width), bf16)]
        + [pltpu.SemaphoreType.DMA((2 * late,))],
        compiler_params=pltpu.CompilerParams(vmem_limit_bytes=(12 * max(1, slot_count // 64) + 4 * late) * MIB),
        cost_estimate=pl.CostEstimate(
            flops=8 * slot_count * width * hid_count, bytes_accessed=4 * width * hid_count, transcendentals=0
        ),
        name="experts",
    )(counts, near_t, far_t, near_g, far_g, column, shift, one, gate, *in_hbm(up, down), *early)


def outer_body(step, left, right, *refs):
    out_h, done, out, sems = refs[-4:]
    done[...] = jnp.zeros_like(done)
    first = refs[-5]
    copies = []
    for k in range(out.shape[0] // step):
        here = pl.ds(k * step, step)
        out[here, :] = dot(left[:, first + k * step : first + (k + 1) * step], right[...], 0, 0).astype(bf16)
        copies += start_copies([(out.at[here], out_h.at[0, pl.ds(first + k * step, step)])], sems.at[pl.ds(k, 1)])
    for copy in copies:
        copy.wait()


def outer(left, right, behind, name, first, count, into=None):
    depth, rows = left.shape
    columns = right.shape[1]
    share = count * rows // 4
    step = min(rows // 4, SHARE // columns)
    before = [] if into is None else [into]

    def body(left, right, _, *refs):
        outer_body(step, left, right, first * rows // 4, *refs[-4:])

    return pl.pallas_call(
        body,
        in_specs=[WHOLE] * 2 + [ORDER] * (1 + len(before)),
        out_specs=[ORDER, WHOLE],
        out_shape=[jax.ShapeDtypeStruct((1, rows, columns), bf16), jax.ShapeDtypeStruct((8, 128), f32)],
        scratch_shapes=[pltpu.VMEM((share, columns), bf16), pltpu.SemaphoreType.DMA((share // step,))],
        input_output_aliases={3: 0} if before else {},
        compiler_params=pltpu.CompilerParams(vmem_limit_bytes=24 * MIB),
        cost_estimate=pl.CostEstimate(
            flops=2 * depth * rows * columns * count, bytes_accessed=rows * columns * count, transcendentals=0
        ),
        name=name,
    )(left, right, behind, *before)


def number_columns(ids, rows):
    blank = jnp.full((SIDE, LANES - ids.shape[1]), -1.0, f32)
    numbers = jnp.concatenate([ids, blank], axis=1)
    return jnp.concatenate([numbers, jnp.zeros((rows - SIDE, LANES), f32)], axis=0)


def fold_body(last, keep_e, keep_b, got_e, got_b, side, ids, _, *outs):
    rows, width = keep_e.shape
    depth = width // LANES
    got = [got_e[...].astype(f32), got_b[...].astype(f32)]
    eo = keep_e[...] + got[0][:, :width]
    back = keep_b[...] + got[1][:, :width]
    theirs = unspread(got[0][:, width:], width) + unspread(got[1][:, width:], width)
    sums = [side[k * depth : (k + 1) * depth] + v for k, v in enumerate(theirs)]
    outs[0][...] = jnp.concatenate(sums, axis=0)
    low, high = slice(0, rows // 2), slice(rows // 2, rows)
    if last:
        mine = jnp.concatenate([eo[low], back[low]], axis=0)
        outs[1][...] = jnp.concatenate([mine, number_columns(ids[:, :rows], rows)], axis=1).astype(bf16)
        send = jnp.concatenate([eo[high], back[high]], axis=0)
        outs[2][...] = jnp.concatenate([send] + [spread(v, rows) for v in sums], axis=1).astype(bf16)
    else:
        outs[1][...] = eo[low]
        outs[2][...] = back[low]
        outs[3][...] = jnp.concatenate([eo[high]] + [spread(v, rows // 2) for v in sums[:2]], axis=1).astype(bf16)
        outs[4][...] = jnp.concatenate([back[high]] + [spread(v, rows // 2) for v in sums[2:]], axis=1).astype(bf16)


def fold(keep, got, side, ids, behind):
    rows, width = keep[0].shape
    last = rows == 2 * MOST
    shapes = [(side.shape, f32)]
    if last:
        shapes += [((rows, width + LANES), bf16), ((rows, width + 4 * spread_columns(width, rows)), bf16)]
    else:
        wide = width + 2 * spread_columns(width, rows // 2)
        shapes += [((rows // 2, width), f32)] * 2 + [((rows // 2, wide), bf16)] * 2
    return pl.pallas_call(
        functools.partial(fold_body, last),
        in_specs=[WHOLE] * 6 + [ORDER],
        out_specs=[WHOLE] * len(shapes),
        out_shape=[jax.ShapeDtypeStruct(shape, kind) for shape, kind in shapes],
        compiler_params=pltpu.CompilerParams(vmem_limit_bytes=16 * MIB),
        name="fold",
    )(*keep, *got, side, ids, behind)


def pack_body(width, got, side, ids, *refs):
    mine_o = refs[-1]
    depth = width // LANES
    theirs = got[...].astype(f32)
    sums = [side[k * depth : (k + 1) * depth] + v for k, v in enumerate(unspread(theirs[:, width:], width)[:3])]
    rows = mine_o.shape[0]
    numbers = number_columns(ids[:, rows:], rows)
    mine_o[...] = jnp.concatenate(
        [theirs[:, :width]] + [spread(v, rows) for v in sums] + [numbers], axis=1
    ).astype(bf16)


def pack(width, got, side, ids, *behind):
    rows = got.shape[0]
    return pl.pallas_call(
        functools.partial(pack_body, width),
        in_specs=[WHOLE] * 3 + [ORDER] * len(behind),
        out_specs=WHOLE,
        out_shape=jax.ShapeDtypeStruct((rows, width + 3 * spread_columns(width, rows) + LANES), bf16),
        compiler_params=pltpu.CompilerParams(vmem_limit_bytes=16 * MIB),
        name="pack",
    )(got, side, ids, *behind)


def relay_body(rows, *refs):
    refs[-1][...] = rows[...]


def relay(rows, *behind):
    return pl.pallas_call(
        relay_body,
        in_specs=[WHOLE] + [ORDER] * len(behind),
        out_specs=WHOLE,
        out_shape=jax.ShapeDtypeStruct(rows.shape, rows.dtype),
        compiler_params=pltpu.CompilerParams(vmem_limit_bytes=16 * MIB),
        name="relay",
    )(rows, *behind)


def normalize_body(tokens, grads, shift, scale, gate, normed_o, inverse_o, tokens_o, grads_o, shift_o, one_o, gate_o):
    inputs = tokens[...].astype(f32)
    centered = inputs - jnp.mean(inputs, axis=1, keepdims=True)
    inverse_std = lax.rsqrt(jnp.mean(centered * centered, axis=1, keepdims=True) + 1e-06)
    normed_o[...] = centered * inverse_std
    inverse_o[...] = jnp.broadcast_to(inverse_std, inverse_o.shape)
    tokens_o[...] = tokens[...]
    grads_o[...] = grads[...]
    shift_o[...] = shift[...]
    one_o[...] = 1.0 + scale[...]
    gate_o[...] = gate[...]


def normalize(tokens, grads, shift, scale, gate):
    tok_count, width = tokens.shape
    step = min(tok_count, 32)
    wide = pl.BlockSpec((step, width), lambda i: (i, 0))
    narrow = pl.BlockSpec((step, 128), lambda i: (i, 0))
    line = pl.BlockSpec((1, width), lambda i: (0, 0))
    return pl.pallas_call(
        normalize_body,
        grid=(tok_count // step,),
        in_specs=[wide, wide, line, line, line],
        out_specs=[wide, narrow, wide, wide, line, line, line],
        out_shape=[
            jax.ShapeDtypeStruct((tok_count, width), f32),
            jax.ShapeDtypeStruct((tok_count, 128), f32),
            jax.ShapeDtypeStruct((tok_count, width), bf16),
            jax.ShapeDtypeStruct((tok_count, width), bf16),
        ]
        + [jax.ShapeDtypeStruct((1, width), f32)] * 3,
        compiler_params=pltpu.CompilerParams(vmem_limit_bytes=16 * MIB),
        cost_estimate=pl.CostEstimate(flops=10 * tok_count * width, bytes_accessed=6 * tok_count * width, transcendentals=0),
        name="normalize",
    )(*in_hbm(tokens, grads, shift, scale, gate))


def finish_body(
    parts, place, side, got, inverse, tokens, grads, normed, one, gate, *refs
):
    pieces = refs[:-14]
    block_h, tgrad_h, gate_h, shift_h, scale_h, router_h = refs[-14:-8]
    gate_s, shift_s, scale_s, router_s, block_s, tgrad_s, vector_sems, out_sems = refs[-8:]
    total = tokens.shape[0]
    count = total // parts
    cuts = [pl.ds(k * count, count) for k in range(parts)]
    width = tokens.shape[1]
    depth = width // LANES
    rows = jnp.concatenate([piece[:, :width] for piece in pieces], axis=0)
    ids = [piece[:, piece.shape[1] - LANES :].astype(f32)[:, : piece.shape[0]] for piece in pieces]
    ids = [jnp.concatenate([each[kind : 1 + kind] for each in ids], axis=1) for kind in range(2)]
    with_sums = [piece for piece in pieces if piece.shape[1] > width + LANES]
    vector = sum(piece[:, width : piece.shape[1] - LANES].astype(f32) for piece in with_sums)
    gate_s[...], shift_s[...], scale_s[...] = unspread(vector, width)
    own = side[3 * depth :]
    other = unspread(got[...].astype(f32)[:, width:], width)[3]
    first = place[1] == 0
    for k, row in enumerate((jnp.where(first, own, other), jnp.where(first, other, own))):
        router_s[k : k + 1] = jnp.concatenate([row[at : at + 1] for at in range(depth)], axis=1)
    departures = start_copies(
        ((gate_s, gate_h), (shift_s, shift_h), (scale_s, scale_h), (router_s, router_h)), vector_sems
    )
    for k, cut in enumerate(cuts):
        numbers = (iota((count, rows.shape[0]), 0) + k * count).astype(f32)
        table = jnp.concatenate([(numbers == each).astype(f32) for each in ids], axis=0)
        sums = dot(table.astype(bf16), rows, 1, 0)
        block_s[cut, :] = (tokens[cut, :].astype(f32) + gate[...] * sums[:count]).astype(bf16)
        grad_norm = sums[count:] * one[...]
        center = jnp.mean(grad_norm, axis=1, keepdims=True)
        along = jnp.mean(grad_norm * normed[cut, :], axis=1, keepdims=True)
        tgrad_s[cut, :] = (
            grads[cut, :].astype(f32) + inverse[cut, 0:1] * (grad_norm - center - normed[cut, :] * along)
        ).astype(bf16)
        departures += start_copies(((block_s.at[cut], block_h.at[cut]), (tgrad_s.at[cut], tgrad_h.at[cut])), out_sems.at[k])
    for copy in departures:
        copy.wait()


def finish(place, side, got, pieces, one, gate, tokens, grads, normed, inverse):
    tok_count, width = tokens.shape
    parts = 4
    vector = jax.ShapeDtypeStruct((width // LANES, LANES), f32)
    return pl.pallas_call(
        functools.partial(finish_body, parts),
        in_specs=[SCALARS] + [WHOLE] * (8 + len(pieces)),
        out_specs=[ORDER] * 6,
        out_shape=[jax.ShapeDtypeStruct((tok_count, width), bf16)] * 2
        + [vector] * 3
        + [jax.ShapeDtypeStruct((2, width), f32)],
        scratch_shapes=[pltpu.VMEM(vector.shape, f32)] * 3
        + [pltpu.VMEM((2, width), f32)]
        + [pltpu.VMEM((tok_count, width), kind) for kind in (bf16, bf16)]
        + [pltpu.SemaphoreType.DMA(shape) for shape in ((4,), (parts, 2))],
        compiler_params=pltpu.CompilerParams(vmem_limit_bytes=24 * MIB),
        name="finish",
    )(place, side, got, inverse, tokens, grads, normed, one, gate, *pieces)


def swap(values, axis, mask):
    size = lax.axis_size(axis)
    return lax.ppermute(values, axis, [(i, i ^ mask) for i in range(size)])


def halvings(size):
    masks = []
    while size > 1:
        size //= 2
        masks.append(size)
    return masks


def per_device(
    tokens, ada_shift, ada_scale, ada_gate, router, expert_up, expert_down, picked_ids, out_grad
):
    tok_count, width = tokens.shape
    ctx_size, exp_size = lax.axis_size("ctx"), lax.axis_size("exp")
    ctx_masks, exp_masks = halvings(ctx_size), halvings(exp_size)
    me = lax.axis_index("ctx")
    group = me // ctx_masks[0]
    picked = picked_ids[0]
    shift, scale, gate = ada_shift[None], ada_scale[None], ada_gate[None]
    place = jnp.stack([me, group]).astype(jnp.int32)
    own, other, ids = select(place, picked_ids, tokens, out_grad)

    orders = ctx_masks[1:], ctx_masks[:0:-1]
    relative = []
    for order in orders:
        blocks = [0]
        for mask in [ctx_masks[0], *order]:
            blocks = blocks + [r ^ mask for r in blocks]
        relative.append(blocks)
    places = [relative[1].index(r) for r in relative[0]]
    sources = me ^ jnp.array(relative[0], jnp.int32)
    own_ids = jnp.where(group == 0, picked[0], picked[1])
    counts = jnp.sum((own_ids // tok_count)[None, :] == sources[:, None], axis=1).astype(jnp.int32)
    columns = router[0].astype(f32).T
    column = jnp.where(group == 0, columns[0:1], columns[1:2])

    normed, inverse, near_tokens, near_grads, shift, one, gate = normalize(tokens, out_grad, shift, scale, gate)
    early, brought, behind = [], 0, own

    def bring_some(step):
        nonlocal brought, behind
        count = min(EARLY[step] if step < len(EARLY) else 0, expert_up.shape[2] // CHUNK - brought)
        if count > 0:
            *weights, behind = bring(expert_up, expert_down, behind, brought, count)
            early.extend(weights)
            brought += count

    got = swap(other, "ctx", ctx_masks[0])
    bring_some(0)
    near = join(True, [own, own], [got, got], behind)
    far = [swap(near[k], "ctx", orders[k][0]) for k in range(2)]
    for step, masks in enumerate(zip(orders[0][1:], orders[1][1:])):
        behind = near[0]
        bring_some(1 + step)
        near = join(False, near, far, behind)
        far = [swap(near[k], "ctx", masks[k]) for k in range(2)]
    behind = near[0]
    bring_some(len(orders[0]))
    hidden, grad_rows, act, grad_pre, eo_keep, back_keep, eo_send, back_send, side = experts(
        places, counts, near[0], far[0], near[1], far[1], shift, one, gate, column, expert_up, expert_down, early
    )

    rows = eo_keep.shape[0]
    keep, send = [eo_keep, back_keep], [eo_send, back_send]
    behind = side
    for step, masks in enumerate(zip(orders[0][::-1], orders[1][::-1])):
        got = [swap(send[k], "ctx", masks[k]) for k in range(2)]
        if step == 0:
            up_grad, behind = outer(hidden, grad_pre, behind, "up_grad", 0, 4)
        elif step == 1:
            down_grad, behind = outer(act, grad_rows, behind, "down_grad", 0, 1)
        side, *rest = fold(keep, got, side, ids, behind)
        keep, send = rest[:-2], rest[-2:]
        behind = side
    mine, send = rest
    got = swap(send, "ctx", ctx_masks[0])
    down_grad, behind = outer(act, grad_rows, behind, "down_grad", 1, 2, down_grad)
    come = swap(mine, "exp", exp_masks[0])
    pieces = [mine, come]
    mine = pack(width, got, side, ids, behind)
    come = swap(mine, "exp", exp_masks[0])
    down_grad, behind = outer(act, grad_rows, mine, "down_grad", 3, 1, down_grad)
    for mask in exp_masks[1:]:
        pieces = pieces + [swap(piece, "exp", mask) for piece in pieces]
    last = [mine, relay(come, behind, *pieces[2:])]
    for mask in exp_masks[1:]:
        last = last + [swap(piece, "exp", mask) for piece in last]
    pieces = pieces + last
    block_out, tokens_grad, gate_grad, shift_grad, scale_grad, router_rows = finish(
        place, side, got, pieces, one, gate, near_tokens, near_grads, normed, inverse
    )
    return (
        block_out,
        tokens_grad,
        up_grad,
        down_grad,
        router_rows.T[None],
        shift_grad.reshape(width),
        scale_grad.reshape(width),
        gate_grad.reshape(width),
    )


def solution(mesh):
    in_specs = (
        P("ctx", None),
        P(),
        P(),
        P(),
        P("exp", None, None),
        P("exp", None, "ctx"),
        P("exp", "ctx", None),
        P("exp", None, None),
        P("ctx", None),
    )
    out_specs = (
        P("ctx", None),
        P("ctx", None),
        P("exp", None, "ctx"),
        P("exp", "ctx", None),
        P("exp", None, None),
        P(),
        P(),
        P(),
    )
    return jax.shard_map(
        per_device, mesh=mesh, in_specs=in_specs, out_specs=out_specs, check_vma=False
    )
```
